512 devices in a mesh: user: 64 (over z, x), item: 4 (over y), rep: 2 (over core).
Axes of the slice: x: 4, y: 4, z: 16, core: 2. Of those that a mesh axis runs over, the one named last changes fastest.
Arguments:
- user_factors: bfloat16 [16384, 256], P('user'), may hold values from -6 to 6
- item_factors: bfloat16 [196608, 256], P(('user', 'item')), may hold values from -6 to 6
- item_bucket: int32 [196608], P(('user', 'item')), may hold values from 0 to 15
- propensity: float32 [16], replicated, may hold values from 0.02 to 1
- tile_blocks: int32 [128, 128], P('user', 'item'), may hold values from 0 to 1535, as said below
- positives: int32 [16384, 128], P('user', 'item'), may hold values from -64 to 127
Outputs:
- new_users: bfloat16 [16384, 256], P('user')
- new_items: bfloat16 [196608, 256], P(('user', 'item'))
The draws below stay inside these ranges and needn't reach their ends.
Inputs may be any that keep to these rules, and one draw needn't show every extreme that they name: `tile_blocks`: column q * 2 * 16 + r * 16 + k (k below 16) of a row names an item block g with (g // 6) % 4 == q. The 32 blocks of one row and one q are distinct and have distinct values of g // 24. Over the 2 rows of one user shard (rows s * 2 to s * 2 + 1) and one q, at most one block of each value of g // 24 is named, and for each q some such value is named in every user shard.
All inputs are finite; a program needn't handle non-finite values.
Results may differ from the reference program's by a relative error of at most 0.015.
Values may be sent and summed in bfloat16 or wider, within the bound.
A program may use at most 64 MiB of HBM per device.

```python
import math
import jax
import jax.numpy as jnp
import numpy as np
from jax import lax

R = 256
BLK = 128
NBUCK = 16
UBD = 2
IBD = 6
KS = 16
KT = 128
ACT = 48
NUB = 128
NU = 16384
NI = 196608
N_USER = 64
N_ITEM = 4
N_REP = 2


def draw_tile_blocks(key, part):
    key = jax.random.fold_in(key, 7)
    subkeys = jax.random.split(key, 4)
    picked_local = jax.random.randint(subkeys[0], (N_USER, N_ITEM, N_USER), 0, IBD)
    hot_owner = jax.random.randint(subkeys[1], (N_ITEM,), 0, N_USER)
    shard_keys = jax.random.split(subkeys[2], N_USER * N_ITEM)
    owner_rank = jax.vmap(lambda subkey: jax.random.permutation(subkey, N_USER))(shard_keys)
    owner_rank = owner_rank.reshape(N_USER, N_ITEM, N_USER)
    owners = jnp.arange(N_USER, dtype=jnp.int32)
    is_hot = owners[None, None, :] == hot_owner[None, :, None]
    active = (owner_rank < ACT - 1) | is_hot
    row_keys = jax.random.split(subkeys[3], N_USER * UBD * N_ITEM)
    row_perm = jax.vmap(lambda subkey: jax.random.permutation(subkey, N_USER))(row_keys)
    row_perm = row_perm.reshape(N_USER, UBD, N_ITEM, N_USER)
    row_score = jnp.where(active[:, None], row_perm, row_perm + N_USER)
    first_row = (jnp.arange(UBD) == 0)[None, :, None, None]
    row_score = jnp.where(first_row & is_hot[:, None], -1, row_score)
    chosen = jnp.argsort(row_score, axis=-1)[..., :N_REP * KS].astype(jnp.int32)
    local_block = jnp.take_along_axis(jnp.broadcast_to(picked_local[:, None], (N_USER, UBD, N_ITEM, N_USER)), chosen, axis=-1)
    group_index = jnp.arange(N_ITEM, dtype=jnp.int32)[None, None, :, None]
    blocks = chosen * (N_ITEM * IBD) + group_index * IBD + local_block
    return blocks.reshape(NUB, N_ITEM * N_REP * KS).astype(jnp.int32)


def place_ends(result, key, smallest, largest):
    longest = result.shape.index(max(result.shape))
    spots = []
    for shift in (0, 1):
        where = [jax.random.randint(jax.random.fold_in(key, axis), (), 0, length) for axis, length in enumerate(result.shape)]
        where[longest] = (where[longest] + shift) % result.shape[longest]
        spots.append(tuple(where))
    return result.at[spots[0]].set(smallest).at[spots[1]].set(largest)


def block_scale(own_key, extent, cuts, least, top_value):
    factor_of, own = 1.0, jax.random.fold_in(own_key, 6)
    for dim, parts in cuts:
        steps = jnp.exp(jax.random.uniform(jax.random.fold_in(own, dim), (parts,), jnp.float32, least / len(cuts), top_value / len(cuts)))
        factor_of = factor_of * jnp.repeat(steps, extent[dim] // parts).reshape([-1 if axis == dim else 1 for axis in range(len(extent))])
    return factor_of


def rank_bounds(count, lean):
    portions = [(1 << 20) // math.isqrt(standing ** lean) + 1 for standing in range(1, count + 1)]
    spread = 1 + sum(portions) // (1 << 30)
    return np.cumsum(np.array([max(1, weight // spread) for weight in portions]))


def skewed_ids(stream_key, dims, count, lean):
    table = rank_bounds(count, lean)
    pick = jax.random.randint(jax.random.fold_in(stream_key, 1), dims, 0, int(table[count - 1]))
    rank = jnp.searchsorted(jnp.asarray(table, jnp.int32), pick, side="right")
    return jax.random.permutation(jax.random.fold_in(stream_key, 2), count)[rank].astype(jnp.int32)


def normal_values(rng, shape, scale, most, pieces=(), kind=jnp.bfloat16):
    result = jax.random.normal(rng, shape, jnp.float32) * scale
    if len(pieces) > 0:
        result = block_scale(rng, shape, pieces, -0.22, 0.18) * result
    return jnp.clip(result, min=-most, max=most).astype(kind)


def setup_inputs(seed: int = 0) -> dict:
    keys = jax.random.split(jax.random.key(seed), 7)
    return {
        "user_factors": normal_values(keys[0], (NU, R), 1.0, 6.0, ((0, 64),)),
        "item_factors": normal_values(keys[1], (NI, R), 1.0, 6.0, ((0, 256),)),
        "item_bucket": place_ends(skewed_ids(keys[2], (NI,), NBUCK, 2), jax.random.fold_in(keys[2], 3), 0, NBUCK - 1).astype(jnp.int32),
        "propensity": jnp.clip(jnp.exp(jax.random.uniform(keys[3], (NBUCK,), jnp.float32, math.log(0.02), math.log(1.0))), 0.02, 1.0),
        "tile_blocks": draw_tile_blocks(jax.random.fold_in(keys[6], 71), 0),
        "positives": place_ends(jax.random.randint(keys[5], (NU, KT), 0 - BLK // 2, BLK), jax.random.fold_in(keys[5], 1), 0 - BLK // 2, BLK - 1).astype(jnp.int32),
    }


STEP_USER = 0.02
STEP_ITEM = 0.1
DECAY = 0.1


def item_hinge(user_block, block_ids, pos_rows, item_blocks, inverse_blocks):
    item_tiles = item_blocks[block_ids]
    inverse_prop = inverse_blocks[block_ids]
    columns = jnp.arange(BLK, dtype=jnp.int32)
    score_scale = R ** -0.5
    raw_scores = jnp.einsum('ar,kjr->kaj', user_block, item_tiles)
    is_positive = pos_rows.T[:, :, None] == columns[None, None, :]
    target_sign = jnp.where(is_positive, 1.0, -1.0).astype(user_block.dtype)
    weight = jnp.where(is_positive, inverse_prop[:, None, :], jnp.ones_like(raw_scores))
    margin = jnp.maximum(1.0 - target_sign * raw_scores * score_scale, 0.0)
    hinge_grad = ((-2.0 * score_scale) * target_sign * weight * margin).astype(jnp.bfloat16)
    hinge_grad = lax.optimization_barrier(hinge_grad).astype(user_block.dtype)
    return hinge_grad, item_tiles


def reference(user_factors, item_factors, item_bucket, propensity, tile_blocks, positives):
    item_blocks = item_factors.astype(jnp.float32).reshape(NI // BLK, BLK, R)
    inverse_blocks = (1.0 / propensity)[item_bucket].reshape(NI // BLK, BLK)
    user_blocks = user_factors.astype(jnp.float32).reshape(NUB, BLK, R)
    pos_blocks = positives.reshape(NUB, BLK, KT)

    def first_pass(inputs):
        user_block, block_ids, pos_rows = inputs
        hinge_grad, item_tiles = item_hinge(user_block, block_ids, pos_rows, item_blocks, inverse_blocks)
        return jnp.einsum('kaj,kjr->ar', hinge_grad, item_tiles)

    user_grad = lax.map(first_pass, (user_blocks, tile_blocks, pos_blocks))
    new_blocks = (user_blocks - STEP_USER * (user_grad + DECAY * user_blocks)).astype(jnp.bfloat16)
    new_float = lax.optimization_barrier(new_blocks).astype(jnp.float32)

    def second_pass(carry, inputs):
        user_block, block_ids, pos_rows = inputs
        hinge_grad, item_tiles = item_hinge(user_block, block_ids, pos_rows, item_blocks, inverse_blocks)
        item_terms = jnp.einsum('kaj,ar->kjr', hinge_grad, user_block)
        return carry.at[block_ids].add(item_terms), None

    item_grad, unused = lax.scan(second_pass, jnp.zeros_like(item_blocks), (new_float, tile_blocks, pos_blocks))
    new_items = (item_blocks - STEP_ITEM * (item_grad + DECAY * item_blocks)).astype(jnp.bfloat16)
    return new_blocks.reshape(NU, R), new_items.reshape(NI, R)
```

```python
import functools

import jax
import jax.numpy as jnp
from jax import lax
from jax.experimental import pallas as pl
from jax.experimental.pallas import tpu as pltpu
from jax.sharding import PartitionSpec as P

BLK = 128
STEP_USER = 0.02
STEP_ITEM = 0.1
DECAY = 0.1
MESH = pl.DeviceIdType.MESH
F32 = jnp.float32
BF16 = jnp.bfloat16

NX = 4
NY = 4
IBD = 6
RANK = 256
HB = IBD // 2
HALF = HB * BLK
QR = BLK // NY


def nt(a, b):
    return lax.dot_general(a, b, (((1,), (1,)), ((), ())), preferred_element_type=F32)


def nn(a, b):
    return lax.dot_general(a, b, (((1,), (0,)), ((), ())), preferred_element_type=F32)


def kernel(nz, u_ref, it_ref, bk_ref, prop_ref, tb_ref, pos_ref, ou_ref, oi_ref,
           cm, cr, idv, ids, items, invp, invrow, invcol, ua, ub, gs, yr, zs_buf, zr, hexp,
           cs, ccr, xs, xr, own_sum,
           c_s, c_r, sm_sem, i_s, i_r, f_s, f_r, p_s, p_r, az_s, az_r, ay_s, ay_r,
           ry_s, ry_r, rz_s, rz_r, bz_s, bz_r, by_s, by_r, g_s, g_r, x_s, x_r, o_s, o_r, l_sem):
    user = lax.axis_index("user")
    y = lax.axis_index("item")
    r = lax.axis_index("rep")
    z = user // NX
    x = user % NX
    c = RANK ** -0.5

    def zdev(zz):
        return (zz * NX + x, y, r)

    def xdev(xx):
        return (z * NX + xx, y, r)

    def ydev(yy):
        return (user, yy, r)

    sib = (user, y, 1 - r)

    def rc(src, dst, ss, rs, dev):
        return pltpu.make_async_remote_copy(
            src_ref=src, dst_ref=dst, send_sem=ss, recv_sem=rs, device_id=dev, device_id_type=MESH)

    def zpeer(i):
        return lax.rem(z + 7 * i, nz)

    def zsrc(i):
        return lax.rem(z + (nz - 7 % nz) * i, nz)

    def off(base, i, n):
        return lax.rem(base + i, n)

    barrier = pltpu.get_barrier_semaphore()

    def greet(i, carry):
        pl.semaphore_signal(barrier, inc=1, device_id=zdev(zpeer(i)), device_id_type=MESH)
        return carry

    lax.fori_loop(1, nz, greet, 0)
    for d in range(1, NX):
        pl.semaphore_signal(barrier, inc=1, device_id=xdev(off(x, d, NX)), device_id_type=MESH)
    for d in range(1, NY):
        pl.semaphore_signal(barrier, inc=1, device_id=ydev(off(y, d, NY)), device_id_type=MESH)
    pl.semaphore_signal(barrier, inc=1, device_id=sib, device_id_type=MESH)

    tb = tb_ref[pl.ds(r, 1), :]
    owner = (tb * 2731) >> 16
    local = tb - owner * (NY * IBD) - y * IBD
    ow_rows = lax.broadcasted_iota(jnp.int32, (nz * NX, tb.shape[1]), 0)
    hot = jnp.where(ow_rows == owner, 1.0, 0.0)
    pos = pos_ref[pl.ds(pl.multiple_of(r * BLK, BLK), BLK), :].astype(F32).astype(BF16)
    pos_by = nt(hot.astype(BF16), pos)
    named = jnp.sum(hot, axis=1, keepdims=True)
    pos_by = jnp.where(named > 0.0, pos_by, -1.0).astype(jnp.int32)
    z_rows = lax.broadcasted_iota(jnp.int32, (nz, tb.shape[1]), 0)
    id_lane = lax.broadcasted_iota(jnp.int32, (nz, BLK), 1)
    id_mat = jnp.zeros((nz, BLK), jnp.int32)
    for xx in range(NX):
        asked = jnp.max(jnp.where(owner == z_rows * NX + xx, local + 1, 0), axis=1, keepdims=True)
        id_mat = jnp.where(id_lane == xx, asked, id_mat)
    for zz in range(nz):
        cm[zz, 0:NX, :] = pos_by[zz * NX:(zz + 1) * NX, :]
        cm[zz, 8:9, :] = id_mat[zz:zz + 1, :]

    bk = bk_ref[...]
    inv = jnp.zeros((IBD, BLK), F32)
    for b in range(16):
        inv = inv + jnp.where(bk == b, 1.0 / jnp.full((IBD, BLK), prop_ref[0, b], F32), 0.0)
    invp[x, 0:IBD, :] = inv * (2.0 * c)

    cr[z] = cm[z]
    ua[z] = u_ref[pl.ds(pl.multiple_of(r * BLK, BLK), BLK), :]
    own_items = pltpu.make_async_copy(it_ref, items.at[x], l_sem)
    own_items.start()

    pl.semaphore_wait(barrier, nz - 1 + NX - 1 + NY - 1 + 1)

    q0 = pl.multiple_of(y * QR, QR)
    h0 = r * HB

    def code_copy(i):
        p = zpeer(i)
        return rc(cm.at[p], cr.at[z], c_s.at[p], c_r.at[z], zdev(p))

    def send_codes(i, carry):
        code_copy(i).start()
        return carry

    def item_copy(d):
        p = off(x, d, NX)
        return rc(it_ref.at[pl.ds(h0, HB)], items.at[x, pl.ds(h0, HB)], i_s.at[p], i_r.at[x], xdev(p))

    def invp_copy(d):
        p = off(x, d, NX)
        return rc(invp.at[x], invp.at[x], p_s.at[p], p_r.at[x], xdev(p))

    def az_copy(i):
        p = zpeer(i)
        return rc(ua.at[z, pl.ds(q0, QR)], ua.at[z, pl.ds(q0, QR)], az_s.at[p], az_r.at[z], zdev(p))

    def send_users(i, carry):
        az_copy(i).start()
        return carry

    for d in (2, 1, 3):
        item_copy(d).start()
    lax.fori_loop(1, nz, send_users, 0)
    lax.fori_loop(1, nz, send_codes, 0)
    for d in (2, 1, 3):
        invp_copy(d).start()

    def forward_y(buf, zz, ss, rs):
        for d in range(1, NY):
            rc(buf.at[zz, pl.ds(q0, QR)], buf.at[zz, pl.ds(q0, QR)], ss.at[zz], rs.at[zz], ydev(off(y, d, NY))).start()

    def three(buf, zz, ss, rs):
        part = buf.at[zz, pl.ds(0, QR * (NY - 1))]
        return rc(part, part, ss.at[zz], rs.at[zz], ydev(off(y, 1, NY)))

    def arrive_z(buf, zz, ss, rs):
        part = buf.at[zz, pl.ds(q0, QR)]
        rc(part, part, ss.at[zz], rs.at[zz], zdev(zz)).wait_recv()

    def forward_first(i, carry):
        zz = zsrc(i)
        arrive_z(ua, zz, az_s, az_r)
        forward_y(ua, zz, ay_s, ay_r)
        return carry

    lax.fori_loop(1, nz, forward_first, 0)

    def sib_items(xx):
        part = items.at[xx, pl.ds(h0, HB)]
        return rc(part, part, f_s.at[xx], f_r.at[xx], sib)

    def sib_items_in(xx):
        part = items.at[xx, pl.ds((1 - r) * HB, HB)]
        return rc(part, part, f_s.at[xx], f_r.at[xx], sib)

    for d in (3, 1, 2):
        xx = off(x, d, NX)
        part = items.at[xx, pl.ds(h0, HB)]
        rc(part, part, i_s.at[xx], i_r.at[xx], xdev(xx)).wait_recv()
        sib_items(xx).start()
    for d in (3, 1, 2):
        xx = off(x, d, NX)
        rc(invp.at[xx], invp.at[xx], p_s.at[xx], p_r.at[xx], xdev(xx)).wait_recv()

    def take_codes(i, carry):
        zz = zsrc(i)
        rc(cm.at[zz], cr.at[zz], c_s.at[zz], c_r.at[zz], zdev(zz)).wait_recv()
        return carry

    lax.fori_loop(1, nz, take_codes, 0)

    for zz in range(nz):
        idv[zz:zz + 1, :] = cr[zz, 8:9, :]
    to_smem = pltpu.make_async_copy(idv, ids, sm_sem)
    to_smem.start()

    for xx in range(NX):
        cols = jnp.transpose(invp[xx])
        for j in range(IBD):
            invcol[xx, j] = jnp.broadcast_to(cols[:, j:j + 1], (BLK, BLK))
            invrow[xx, j] = jnp.broadcast_to(invp[xx, j:j + 1, :], (8, BLK))

    to_smem.wait()
    own_items.wait()
    for d in (3, 1, 2):
        sib_items_in(off(x, d, NX)).wait_recv()

    lane = lax.broadcasted_iota(jnp.int32, (BLK, BLK), 1)
    lane_f = lane.astype(F32)
    sub = lax.broadcasted_iota(jnp.int32, (BLK, BLK), 0)

    def pick(zz, xx):
        code = ids[zz, xx]
        j = jnp.maximum(code - 1, 0)
        block = items[xx, j]
        flat = jnp.where(code > 0, 2.0 * c, 0.0).astype(F32)
        return code, j, block, flat

    def grads(zz):
        users = ua[zz]
        cols = jnp.transpose(cr[zz, 0:8, :].astype(F32))
        blocks, hs = [], []
        picks = [pick(zz, xx) for xx in range(NX)]
        stack = jnp.concatenate([p[2] for p in picks], axis=0)
        scores = nt(users, stack)
        for xx in range(NX):
            code, j, block, flat = picks[xx]
            s = scores[:, xx * BLK:(xx + 1) * BLK]
            hit = cols[:, xx:xx + 1] == lane_f
            w = invrow[xx, j][0:1, :]
            m = jnp.maximum(1.0 + s * jnp.where(hit, -c, c), 0.0)
            hs.append((m * jnp.where(hit, -w, flat)).astype(BF16))
        return nn(jnp.concatenate(hs, axis=1), stack)

    def ry_copy(zz, d):
        p = off(y, d, NY)
        return rc(gs.at[zz, pl.ds(pl.multiple_of(p * QR, QR), QR)], yr.at[zz, pl.ds(q0, QR)],
                  ry_s.at[zz], ry_r.at[zz], ydev(p))

    def first_pass(i, carry):
        zz = zsrc(i)

        @pl.when(i > 0)
        def _():
            three(ua, zz, ay_s, ay_r).wait_recv()

        gs[zz] = grads(zz).astype(BF16)
        for d in (2, 1, 3):
            ry_copy(zz, d).start()
        return carry

    lax.fori_loop(0, nz, first_pass, 0)

    def rz_copy(zz):
        return rc(zs_buf.at[zz], zr.at[z], rz_s.at[zz], rz_r.at[z], zdev(zz))

    def sum_y(zz):
        part = yr.at[zz, pl.ds(0, QR * (NY - 1))]
        rc(part, part, ry_s.at[zz], ry_r.at[zz], ydev(off(y, 1, NY))).wait_recv()
        total = gs[zz, pl.ds(q0, QR), :].astype(F32)
        for d in range(1, NY):
            total = total + yr[zz, pl.ds(pl.multiple_of(off(y, d, NY) * QR, QR), QR), :].astype(F32)
        return total

    own_sum[...] = sum_y(z)

    def second_sum(i, carry):
        zz = zsrc(i)
        zs_buf[zz] = sum_y(zz).astype(BF16)
        rz_copy(zz).start()
        return carry

    lax.fori_loop(1, nz, second_sum, 0)

    def gather_sum(i, carry):
        zz = zsrc(i)
        rc(zs_buf.at[zz], zr.at[zz], rz_s.at[zz], rz_r.at[zz], zdev(zz)).wait_recv()
        own_sum[...] += zr[zz].astype(F32)
        return carry

    lax.fori_loop(1, nz, gather_sum, 0)

    old = u_ref[pl.ds(pl.multiple_of(r * BLK + q0, QR), QR), :].astype(F32)
    ub[z, pl.ds(q0, QR), :] = (old - STEP_USER * (own_sum[...] + DECAY * old)).astype(BF16)

    def bz_copy(i):
        p = zpeer(i)
        return rc(ub.at[z, pl.ds(q0, QR)], ub.at[z, pl.ds(q0, QR)], bz_s.at[p], bz_r.at[z], zdev(p))

    def send_new(i, carry):
        bz_copy(i).start()
        return carry

    lax.fori_loop(1, nz, send_new, 0)
    forward_y(ub, z, by_s, by_r)

    def forward_second(i, carry):
        zz = zsrc(i)
        arrive_z(ub, zz, bz_s, bz_r)
        forward_y(ub, zz, by_s, by_r)
        return carry

    def expand(zz):
        users = ub[zz]
        z0 = pl.multiple_of(zz * BLK, BLK)
        for xx in range(NX):
            code, j, block, flat = pick(zz, xx)
            s = nt(block, users)
            hit = cr[zz, xx:xx + 1, :] == sub
            m = jnp.maximum(1.0 + s * jnp.where(hit, -c, c), 0.0)
            h = m * jnp.where(hit, -invcol[xx, j], flat)
            for jj in range(IBD):
                hexp[xx, jj * BLK:(jj + 1) * BLK, pl.ds(z0, BLK)] = jnp.where(code == jj + 1, h, 0.0).astype(BF16)

    LAG = 3

    def second_pass(i, carry):
        @pl.when(jnp.logical_and(i > 0, i < nz))
        def _():
            forward_second(i, 0)

        @pl.when(i >= LAG)
        def _():
            zz = zsrc(i - LAG)
            three(ub, zz, by_s, by_r).wait_recv()
            expand(zz)

        return carry

    lax.fori_loop(0, nz + LAG, second_pass, 0)

    b0 = pl.multiple_of(r * BLK, BLK)
    ou_ref[pl.ds(b0, BLK), :] = ub[z]
    out_u = rc(ub.at[z], ou_ref.at[pl.ds(b0, BLK)], o_s.at[0], o_r.at[0], sib)
    out_u.start()

    flat_users = ub.reshape(nz * BLK, RANK)

    def item_dot(xx, h):
        rows = hexp[xx, pl.ds(pl.multiple_of(h * HALF, HALF), HALF), :]
        return nn(rows, flat_users[...])

    def core_copy(xx):
        return rc(cs.at[xx], ccr.at[xx], g_s.at[xx], g_r.at[xx], sib)

    def other_half(k, carry):
        xx = lax.rem(x + k + 1, NX)
        cs[xx] = item_dot(xx, 1 - r).astype(BF16)
        core_copy(xx).start()
        return carry

    lax.fori_loop(0, NX, other_half, 0)

    def x_copy(xx):
        return rc(xs.at[xx], xr.at[x], x_s.at[xx], x_r.at[x], xdev(xx))

    def own_half(k, carry):
        xx = lax.rem(x + k + 1, NX)
        mine = item_dot(xx, r)
        core_copy(xx).wait_recv()
        xs[xx] = (mine + ccr[xx].astype(F32)).astype(BF16)

        @pl.when(k < NX - 1)
        def _():
            x_copy(xx).start()

        return carry

    lax.fori_loop(0, NX, own_half, 0)
    total = xs[x].astype(F32)
    for d in (1, 3, 2):
        xx = off(x, d, NX)
        rc(xs.at[xx], xr.at[xx], x_s.at[xx], x_r.at[xx], xdev(xx)).wait_recv()
        total = total + xr[xx].astype(F32)
    olds = it_ref[pl.ds(h0, HB)].astype(F32)
    total = total.reshape(HB, BLK, RANK)
    oi_ref[pl.ds(h0, HB)] = (olds - STEP_ITEM * (total + DECAY * olds)).astype(BF16)
    out_i = rc(oi_ref.at[pl.ds(h0, HB)], oi_ref.at[pl.ds(h0, HB)], o_s.at[1], o_r.at[1], sib)
    out_i.start()

    for d in (2, 1, 3):
        item_copy(d).wait_send()
        invp_copy(d).wait_send()
        xx = off(x, d, NX)
        sib_items(xx).wait_send()
        x_copy(xx).wait_send()
    for d in range(NX):
        core_copy(off(x, d, NX)).wait_send()

    def sent(i, carry):
        code_copy(i).wait_send()
        az_copy(i).wait_send()
        bz_copy(i).wait_send()
        zz = zsrc(i)
        three(ua, zz, ay_s, ay_r).wait_send()
        rz_copy(zz).wait_send()
        return carry

    lax.fori_loop(1, nz, sent, 0)

    def sent_all(i, carry):
        three(ub, i, by_s, by_r).wait_send()
        three(gs, i, ry_s, ry_r).wait_send()
        return carry

    lax.fori_loop(0, nz, sent_all, 0)
    out_u.wait_send()
    out_i.wait_send()
    other_b = pl.multiple_of((1 - r) * BLK, BLK)
    other_h = (1 - r) * HB
    rc(ub.at[z], ou_ref.at[pl.ds(other_b, BLK)], o_s.at[0], o_r.at[0], sib).wait_recv()
    rc(oi_ref.at[pl.ds(other_h, HB)], oi_ref.at[pl.ds(other_h, HB)], o_s.at[1], o_r.at[1], sib).wait_recv()


def body(nz, user_factors, item_factors, item_bucket, propensity, tile_blocks, positives):
    dma = pltpu.SemaphoreType.DMA
    V = pltpu.VMEM
    scratch = [
        V((nz, 16, BLK), jnp.int32),
        V((nz, 16, BLK), jnp.int32),
        V((nz, BLK), jnp.int32),
        pltpu.SMEM((nz, BLK), jnp.int32),
        V((NX, IBD, BLK, RANK), BF16),
        V((NX, 8, BLK), F32),
        V((NX, IBD, 8, BLK), F32),
        V((NX, IBD, BLK, BLK), F32),
        V((nz, BLK, RANK), BF16),
        V((nz, BLK, RANK), BF16),
        V((nz, BLK, RANK), BF16),
        V((nz, BLK, RANK), BF16),
        V((nz, QR, RANK), BF16),
        V((nz, QR, RANK), BF16),
        V((NX, IBD * BLK, nz * BLK), BF16),
        V((NX, HALF, RANK), BF16),
        V((NX, HALF, RANK), BF16),
        V((NX, HALF, RANK), BF16),
        V((NX, HALF, RANK), BF16),
        V((QR, RANK), F32),
        dma((nz,)), dma((nz,)), dma,
        dma((NX,)), dma((NX,)), dma((NX,)), dma((NX,)), dma((NX,)), dma((NX,)),
        dma((nz,)), dma((nz,)), dma((nz,)), dma((nz,)),
        dma((nz,)), dma((nz,)), dma((nz,)), dma((nz,)),
        dma((nz,)), dma((nz,)), dma((nz,)), dma((nz,)),
        dma((NX,)), dma((NX,)), dma((NX,)), dma((NX,)),
        dma((2,)), dma((2,)), dma,
    ]
    vmem = pl.BlockSpec(memory_space=pltpu.VMEM)
    new_users, new_items = pl.pallas_call(
        functools.partial(kernel, nz),
        out_shape=(
            jax.ShapeDtypeStruct(user_factors.shape, BF16),
            jax.ShapeDtypeStruct((IBD, BLK, RANK), BF16),
        ),
        in_specs=[vmem, vmem, vmem, pl.BlockSpec(memory_space=pltpu.SMEM), vmem, vmem],
        out_specs=(vmem, vmem),
        scratch_shapes=scratch,
        compiler_params=pltpu.CompilerParams(
            collective_id=0, has_side_effects=True, vmem_limit_bytes=56 << 20),
    )(
        user_factors,
        item_factors.reshape(IBD, BLK, RANK),
        item_bucket.reshape(IBD, BLK),
        propensity.reshape(1, -1),
        tile_blocks,
        positives,
    )
    return new_users, new_items.reshape(item_factors.shape)


def solution(mesh):
    nz = mesh.shape["user"] // NX
    return jax.shard_map(
        functools.partial(body, nz),
        mesh=mesh,
        in_specs=(
            P("user", None),
            P(("user", "item"), None),
            P(("user", "item")),
            P(),
            P("user", "item"),
            P("user", "item"),
        ),
        out_specs=(P("user", None), P(("user", "item"), None)),
        check_vma=False,
    )
```

```python
import functools

import jax
import jax.numpy as jnp
from jax import lax
from jax.experimental import pallas as pl
from jax.experimental.pallas import tpu as pltpu
from jax.sharding import PartitionSpec as P

BLK = 128
STEP_USER = 0.02
STEP_ITEM = 0.1
DECAY = 0.1
MESH = pl.DeviceIdType.MESH
F32 = jnp.float32
BF16 = jnp.bfloat16

NX = 4
NY = 4
IBD = 6
RANK = 256
HB = IBD // 2
HALF = HB * BLK
QR = BLK // NY
NO = 2 * NX
ZB = 2
ZB2 = 2
ZROWS = ZB2 * BLK
LAG1 = 4
LAG2 = 3


def nt(a, b):
    return lax.dot_general(a, b, (((1,), (1,)), ((), ())), preferred_element_type=F32)


def nn(a, b):
    return lax.dot_general(a, b, (((1,), (0,)), ((), ())), preferred_element_type=F32)


def kernel(na, u_ref, it_ref, bk_ref, prop_ref, tb_ref, pos_ref, ou_ref, oi_ref,
           cm, cr, idv, ids, items, invp, invrow, invcol, ua, ub, gs, yr, zs_buf, zr, hexp,
           cs, ccr, xs, zrec, xrec, xrec1, psum, prec, own_sum,
           c_s, c_r, sm_sem, ix_s, ix_r, iz_s, iz_r, jx_s, jx_r, jz_s, jz_r, f_s, f_r,
           p_s, p_r, pz_s, pz_r, pf_s, pf_r,
           az_s, az_r, ay_s, ay_r, ry_s, ry_r, rz_s, rz_r, bz_s, bz_r, by_s, by_r,
           g_s, g_r, x_s, x_r, w_s, w_r, v_s, v_r, t_s, t_r, o_s, o_r, l_sem):
    user = lax.axis_index("user")
    y = lax.axis_index("item")
    r = lax.axis_index("rep")
    z = user // NX
    x = user % NX
    m = z // 2
    p = z % 2
    own = NX * p
    far = NX - own
    k0 = own + x
    c = RANK ** -0.5

    def zdev(mm):
        return ((2 * mm + p) * NX + x, y, r)

    def xdev(xx):
        return (z * NX + xx, y, r)

    def ydev(yy):
        return (user, yy, r)

    sib = (user, y, 1 - r)
    mate = ((2 * m + 1 - p) * NX + x, y, r)

    def rc(src, dst, ss, rs, dev):
        return pltpu.make_async_remote_copy(
            src_ref=src, dst_ref=dst, send_sem=ss, recv_sem=rs, device_id=dev, device_id_type=MESH)

    def step(i):
        return na // 2 + (2 * (i % 2) - 1) * ((i + 1) // 2)

    def peer(i):
        return lax.rem(m + step(i), na)

    def source(i):
        return lax.rem(m + 2 * na - step(i), na)

    def off(base, i, n):
        return lax.rem(base + i, n)

    barrier = pltpu.get_barrier_semaphore()

    def greet(i, carry):
        pl.semaphore_signal(barrier, inc=1, device_id=zdev(peer(i)), device_id_type=MESH)
        return carry

    lax.fori_loop(0, na - 1, greet, 0)
    for d in range(1, NX):
        pl.semaphore_signal(barrier, inc=1, device_id=xdev(off(x, d, NX)), device_id_type=MESH)
    for d in range(1, NY):
        pl.semaphore_signal(barrier, inc=1, device_id=ydev(off(y, d, NY)), device_id_type=MESH)
    pl.semaphore_signal(barrier, inc=1, device_id=sib, device_id_type=MESH)
    pl.semaphore_signal(barrier, inc=1, device_id=mate, device_id_type=MESH)

    b0 = pl.multiple_of(r * BLK, BLK)
    q0 = pl.multiple_of(y * QR, QR)
    h0 = r * HB
    own_items = pltpu.make_async_copy(it_ref, items.at[k0], l_sem.at[0])
    own_items.start()
    own_users = pltpu.make_async_copy(u_ref.at[pl.ds(b0, BLK)], ua.at[m], l_sem.at[1])
    own_users.start()

    tb = tb_ref[pl.ds(r, 1), :]
    owner = (tb * 2731) >> 16
    local = tb - owner * (NY * IBD) - y * IBD
    ow_rows = lax.broadcasted_iota(jnp.int32, (na * NO, tb.shape[1]), 0)
    hot = jnp.where(ow_rows == owner, 1.0, 0.0)
    pos = pos_ref[:, pl.ds(b0, BLK)].astype(F32).astype(BF16)
    pos_by = nn(hot.astype(BF16), pos)
    named = jnp.sum(hot, axis=1, keepdims=True)
    pos_by = jnp.where(named > 0.0, pos_by, -1.0).astype(jnp.int32)
    m_rows = lax.broadcasted_iota(jnp.int32, (na, tb.shape[1]), 0)
    id_lane = lax.broadcasted_iota(jnp.int32, (na, BLK), 1)
    id_mat = jnp.zeros((na, BLK), jnp.int32)
    for k in range(NO):
        asked = jnp.max(jnp.where(owner == m_rows * NO + k, local + 1, 0), axis=1, keepdims=True)
        id_mat = jnp.where(id_lane == k, asked, id_mat)
    for mm in range(na):
        cm[mm, 0:NO, :] = pos_by[mm * NO:(mm + 1) * NO, :]
        cm[mm, NO:NO + 1, :] = id_mat[mm:mm + 1, :]

    bk = bk_ref[...]
    inv = jnp.zeros((IBD, BLK), F32)
    for b in range(16):
        inv = inv + jnp.where(bk == b, 1.0 / jnp.full((IBD, BLK), prop_ref[0, b], F32), 0.0)
    invp[k0, 0:IBD, :] = inv * (2.0 * c)
    cr[m] = cm[m]

    def code_copy(i):
        mm = peer(i)
        return rc(cm.at[mm], cr.at[m], c_s.at[mm], c_r.at[m], zdev(mm))

    def az_copy(i):
        mm = peer(i)
        part = ua.at[m, pl.ds(q0, QR)]
        return rc(part, part, az_s.at[mm], az_r.at[m], zdev(mm))

    def ix_copy(xx):
        part = items.at[k0, pl.ds(h0, HB)]
        return rc(part, part, ix_s.at[xx], ix_r.at[x], xdev(xx))

    def ix_in(xx):
        part = items.at[own + xx, pl.ds(h0, HB)]
        return rc(part, part, ix_s.at[xx], ix_r.at[xx], xdev(xx))

    def iz_copy(k):
        part = items.at[k, pl.ds(h0, HB)]
        return rc(part, part, iz_s, iz_r, mate)

    def jz_copy(k, xx):
        part = items.at[k, pl.ds(h0 + ZB, HB - ZB)]
        return rc(part, part, jz_s.at[xx], jz_r.at[xx], mate)

    def jx_copy(xx):
        part = items.at[far + x, pl.ds(h0, ZB)]
        return rc(part, part, jx_s.at[xx], jx_r.at[x], xdev(xx))

    def jx_in(xx):
        part = items.at[far + xx, pl.ds(h0, ZB)]
        return rc(part, part, jx_s.at[xx], jx_r.at[xx], xdev(xx))

    def core_items(k, start):
        part = items.at[k, pl.ds(start, HB)]
        return rc(part, part, f_s.at[k], f_r.at[k], sib)

    def p_copy(k, xx, ss, rs, slot):
        return rc(invp.at[k], invp.at[k], ss.at[xx], rs.at[slot], xdev(xx))

    def pz_copy(k):
        return rc(invp.at[k], invp.at[k], pz_s, pz_r, mate)

    own_users.wait()
    own_items.wait()
    pl.semaphore_wait(barrier, na - 1 + NX - 1 + NY - 1 + 2)

    def send_users(i, carry):
        az_copy(i).start()
        return carry

    def send_codes(i, carry):
        code_copy(i).start()
        return carry

    for d in (2, 1, 3):
        ix_copy(off(x, d, NX)).start()
    lax.fori_loop(0, na - 1, send_users, 0)
    iz_copy(k0).start()
    lax.fori_loop(0, na - 1, send_codes, 0)
    for d in (2, 1, 3):
        xx = off(x, d, NX)
        p_copy(k0, xx, p_s, p_r, x).start()
    pz_copy(k0).start()

    def forward_y(buf, mm, ss, rs):
        part = buf.at[mm, pl.ds(q0, QR)]
        for d in (2, 1, 3):
            rc(part, part, ss.at[mm], rs.at[mm], ydev(off(y, d, NY))).start()

    def three(buf, mm, ss, rs):
        part = buf.at[mm, pl.ds(0, QR * (NY - 1))]
        return rc(part, part, ss.at[mm], rs.at[mm], ydev(off(y, 1, NY)))

    def arrive_z(buf, mm, ss, rs):
        part = buf.at[mm, pl.ds(q0, QR)]
        rc(part, part, ss.at[mm], rs.at[mm], zdev(mm)).wait_recv()

    def forward_first(i, carry):
        mm = source(na - 2 - i)
        arrive_z(ua, mm, az_s, az_r)
        forward_y(ua, mm, ay_s, ay_r)
        return carry

    lax.fori_loop(0, 4, forward_first, 0)
    iz_copy(far + x).wait_recv()
    for d in (2, 1, 3):
        jx_copy(off(x, d, NX)).start()
    core_items(far + x, h0).start()
    lax.fori_loop(4, na - 1, forward_first, 0)
    pz_copy(far + x).wait_recv()
    for d in (2, 1, 3):
        xx = off(x, d, NX)
        p_copy(far + x, xx, pf_s, pf_r, x).start()
    for d in (1, 3, 2):
        xx = off(x, d, NX)
        ix_in(xx).wait_recv()
        jz_copy(own + xx, xx).start()
        core_items(own + xx, h0).start()
    for d in (1, 3, 2):
        xx = off(x, d, NX)
        p_copy(own + xx, xx, p_s, p_r, xx).wait_recv()
        p_copy(far + xx, xx, pf_s, pf_r, xx).wait_recv()

    def take_codes(i, carry):
        mm = source(i)
        rc(cm.at[mm], cr.at[mm], c_s.at[mm], c_r.at[mm], zdev(mm)).wait_recv()
        return carry

    lax.fori_loop(0, na - 1, take_codes, 0)
    for mm in range(na):
        idv[mm:mm + 1, :] = cr[mm, NO:NO + 1, :]
    to_smem = pltpu.make_async_copy(idv, ids, sm_sem)
    to_smem.start()
    for k in range(NO):
        cols = jnp.transpose(invp[k])
        for j in range(IBD):
            invcol[k, j] = jnp.broadcast_to(cols[:, j:j + 1], (BLK, BLK))
            invrow[k, j] = jnp.broadcast_to(invp[k, j:j + 1, :], (8, BLK))
    for d in (1, 3, 2):
        xx = off(x, d, NX)
        jx_in(xx).wait_recv()
        jz_copy(far + xx, xx).wait_recv()
        core_items(far + xx, h0).start()
    to_smem.wait()
    o0 = (1 - r) * HB
    core_items(far + x, o0).wait_recv()
    for d in (1, 3, 2):
        xx = off(x, d, NX)
        core_items(own + xx, o0).wait_recv()
        core_items(far + xx, o0).wait_recv()

    lane_f = lax.broadcasted_iota(jnp.int32, (BLK, BLK), 1).astype(F32)
    sub = lax.broadcasted_iota(jnp.int32, (BLK, BLK), 0)

    def pick(mm, k):
        code = ids[mm, k]
        j = jnp.maximum(code - 1, 0)
        flat = jnp.where(code > 0, 2.0 * c, 0.0).astype(F32)
        return code, j, items[k, j], flat

    def grads(mm):
        users = ua[mm]
        cols = jnp.transpose(cr[mm, 0:NO, :].astype(F32))
        total = jnp.zeros((BLK, RANK), F32)
        for part in range(NO // NX):
            picks = [pick(mm, part * NX + q) for q in range(NX)]
            stack = jnp.concatenate([t[2] for t in picks], axis=0)
            scores = nt(users, stack)
            hs = []
            for q in range(NX):
                k = part * NX + q
                code, j, block, flat = picks[q]
                s = scores[:, q * BLK:(q + 1) * BLK]
                hit = cols[:, k:k + 1] == lane_f
                w = invrow[k, j][0:1, :]
                margin = jnp.maximum(1.0 + s * jnp.where(hit, -c, c), 0.0)
                hs.append((margin * jnp.where(hit, -w, flat)).astype(BF16))
            total = total + nn(jnp.concatenate(hs, axis=1), stack)
        return total

    def ry_copy(mm, d):
        yy = off(y, d, NY)
        return rc(gs.at[mm, pl.ds(pl.multiple_of(yy * QR, QR), QR)], yr.at[mm, pl.ds(q0, QR)],
                  ry_s.at[mm], ry_r.at[mm], ydev(yy))

    def rz_copy(mm):
        return rc(zs_buf.at[mm], zr.at[m], rz_s.at[mm], rz_r.at[m], zdev(mm))

    def sum_y(mm):
        part = yr.at[mm, pl.ds(0, QR * (NY - 1))]
        rc(part, part, ry_s.at[mm], ry_r.at[mm], ydev(off(y, 1, NY))).wait_recv()
        total = gs[mm, pl.ds(q0, QR), :].astype(F32)
        for d in range(1, NY):
            total = total + yr[mm, pl.ds(pl.multiple_of(off(y, d, NY) * QR, QR), QR), :].astype(F32)
        return total

    def first_pass(i, carry):
        @pl.when(i < na)
        def _():
            mm = peer(i)

            @pl.when(i < na - 1)
            def _():
                three(ua, mm, ay_s, ay_r).wait_recv()

            gs[mm] = grads(mm).astype(BF16)
            for d in (2, 1, 3):
                ry_copy(mm, d).start()

        @pl.when(i >= LAG1)
        def _():
            mm = peer(i - LAG1)
            total = sum_y(mm)

            @pl.when(i < na - 1 + LAG1)
            def _():
                zs_buf[mm] = total.astype(BF16)
                rz_copy(mm).start()

            @pl.when(i == na - 1 + LAG1)
            def _():
                own_sum[...] = total

        return carry

    lax.fori_loop(0, na + LAG1, first_pass, 0)

    def gather_sum(i, carry):
        mm = source(i)
        rc(zs_buf.at[mm], zr.at[mm], rz_s.at[mm], rz_r.at[mm], zdev(mm)).wait_recv()
        own_sum[...] += zr[mm].astype(F32)
        return carry

    lax.fori_loop(0, na - 1, gather_sum, 0)

    old = ua[m, pl.ds(q0, QR), :].astype(F32)
    ub[m, pl.ds(q0, QR), :] = (old - STEP_USER * (own_sum[...] + DECAY * old)).astype(BF16)

    def bz_copy(i):
        mm = peer(i)
        part = ub.at[m, pl.ds(q0, QR)]
        return rc(part, part, bz_s.at[mm], bz_r.at[m], zdev(mm))

    def send_new(i, carry):
        bz_copy(i).start()
        return carry

    lax.fori_loop(0, na - 1, send_new, 0)
    forward_y(ub, m, by_s, by_r)

    def expand(mm):
        users = ub[mm]
        z0 = pl.multiple_of(mm * BLK, BLK)
        for k in range(NO):
            code, j, block, flat = pick(mm, k)
            s = nt(block, users)
            hit = cr[mm, k:k + 1, :] == sub
            margin = jnp.maximum(1.0 + s * jnp.where(hit, -c, c), 0.0)
            h = margin * jnp.where(hit, -invcol[k, j], flat)
            for jj in range(IBD):
                hexp[k, jj * BLK:(jj + 1) * BLK, pl.ds(z0, BLK)] = jnp.where(code == jj + 1, h, 0.0).astype(BF16)

    def second_pass(i, carry):
        @pl.when(jnp.logical_and(i > 0, i < na))
        def _():
            mm = source(na - 1 - i)
            arrive_z(ub, mm, bz_s, bz_r)
            forward_y(ub, mm, by_s, by_r)

        @pl.when(i >= LAG2)
        def _():
            mm = source(na - 1 - (i - LAG2))
            three(ub, mm, by_s, by_r).wait_recv()
            expand(mm)

        return carry

    lax.fori_loop(0, na + LAG2, second_pass, 0)

    ou_ref[pl.ds(b0, BLK), :] = ub[m]
    out_u = rc(ub.at[m], ou_ref.at[pl.ds(b0, BLK)], o_s.at[0], o_r.at[0], sib)
    out_u.start()

    flat_users = ub.reshape(na * BLK, RANK)

    def item_dot(k, h):
        rows = hexp[k, pl.ds(pl.multiple_of(h * HALF, HALF), HALF), :]
        return nn(rows, flat_users[...])

    def core_copy(k):
        return rc(cs.at[k], ccr.at[k], g_s.at[k], g_r.at[k], sib)

    def other_half(j, carry):
        k = lax.rem(far + NX * (j // NX), NO) + lax.rem(x + 1 + j, NX)
        cs[k] = item_dot(k, 1 - r).astype(BF16)
        core_copy(k).start()
        return carry

    lax.fori_loop(0, NO, other_half, 0)

    def w_copy(xx):
        return rc(xs.at[far + xx, pl.ds(0, ZROWS)], zrec.at[xx], w_s.at[xx], w_r.at[xx], mate)

    def w_in(xx):
        return rc(xs.at[own + xx, pl.ds(0, ZROWS)], zrec.at[xx], w_s.at[xx], w_r.at[xx], mate)

    def v_copy(xx):
        return rc(xs.at[far + xx, pl.ds(ZROWS, HALF - ZROWS)], xrec1.at[x], v_s.at[xx], v_r.at[x], xdev(xx))

    def x_copy(xx):
        return rc(xs.at[own + xx], xrec.at[x], x_s.at[xx], x_r.at[x], xdev(xx))

    def far_half(j, carry):
        xx = lax.rem(x + 1 + j, NX)
        k = far + xx
        mine = item_dot(k, r)
        core_copy(k).wait_recv()
        xs[k] = (mine + ccr[k].astype(F32)).astype(BF16)
        w_copy(xx).start()

        @pl.when(j < NX - 1)
        def _():
            v_copy(xx).start()

        return carry

    lax.fori_loop(0, NX, far_half, 0)

    def own_half(j, carry):
        xx = lax.rem(x + 1 + j, NX)
        k = own + xx
        mine = item_dot(k, r)
        core_copy(k).wait_recv()
        w_in(xx).wait_recv()
        total = mine + ccr[k].astype(F32)
        xs[k, pl.ds(0, ZROWS), :] = (total[0:ZROWS] + zrec[xx].astype(F32)).astype(BF16)
        xs[k, pl.ds(ZROWS, HALF - ZROWS), :] = total[ZROWS:].astype(BF16)

        @pl.when(j < NX - 1)
        def _():
            x_copy(xx).start()

        return carry

    lax.fori_loop(0, NX, own_half, 0)

    part = xs[far + x, pl.ds(ZROWS, HALF - ZROWS), :].astype(F32)
    for d in (1, 3, 2):
        xx = off(x, d, NX)
        rc(xrec1.at[xx], xrec1.at[xx], v_s.at[xx], v_r.at[xx], xdev(xx)).wait_recv()
        part = part + xrec1[xx].astype(F32)
    psum[...] = part.astype(BF16)
    to_mate = rc(psum, prec, t_s, t_r, mate)
    to_mate.start()

    for d in (1, 3, 2):
        xx = off(x, d, NX)
        rc(xrec.at[xx], xrec.at[xx], x_s.at[xx], x_r.at[xx], xdev(xx)).wait_recv()
    to_mate.wait_recv()
    for b in range(HB):
        rows = pl.ds(b * BLK, BLK)
        total = xs[k0, rows, :].astype(F32)
        for d in range(1, NX):
            total = total + xrec[off(x, d, NX), rows, :].astype(F32)
        if b >= ZB2:
            total = total + prec[pl.ds((b - ZB2) * BLK, BLK), :].astype(F32)
        olds = items[k0, h0 + b].astype(F32)
        oi_ref[h0 + b] = (olds - STEP_ITEM * (total + DECAY * olds)).astype(BF16)
    mine = oi_ref.at[pl.ds(h0, HB)]
    out_i = rc(mine, mine, o_s.at[1], o_r.at[1], sib)
    out_i.start()

    iz_copy(k0).wait_send()
    pz_copy(k0).wait_send()
    to_mate.wait_send()
    core_items(far + x, h0).wait_send()
    for d in range(NX):
        xx = off(x, d, NX)
        core_copy(own + xx).wait_send()
        core_copy(far + xx).wait_send()
        w_copy(xx).wait_send()
        if d:
            ix_copy(xx).wait_send()
            jx_copy(xx).wait_send()
            jz_copy(own + xx, xx).wait_send()
            core_items(own + xx, h0).wait_send()
            core_items(far + xx, h0).wait_send()
            p_copy(k0, xx, p_s, p_r, x).wait_send()
            p_copy(far + x, xx, pf_s, pf_r, x).wait_send()
            v_copy(xx).wait_send()
            x_copy(xx).wait_send()

    def sent(i, carry):
        code_copy(i).wait_send()
        az_copy(i).wait_send()
        bz_copy(i).wait_send()
        mm = peer(i)
        three(ua, mm, ay_s, ay_r).wait_send()
        rz_copy(mm).wait_send()
        return carry

    lax.fori_loop(0, na - 1, sent, 0)

    def sent_all(i, carry):
        three(ub, i, by_s, by_r).wait_send()
        three(gs, i, ry_s, ry_r).wait_send()
        return carry

    lax.fori_loop(0, na, sent_all, 0)
    out_u.wait_send()
    out_i.wait_send()
    other_b = pl.multiple_of((1 - r) * BLK, BLK)
    rc(ub.at[m], ou_ref.at[pl.ds(other_b, BLK)], o_s.at[0], o_r.at[0], sib).wait_recv()
    theirs = oi_ref.at[pl.ds(o0, HB)]
    rc(theirs, theirs, o_s.at[1], o_r.at[1], sib).wait_recv()


def body(na, user_factors, item_factors, item_bucket, propensity, tile_blocks, positives):
    dma = pltpu.SemaphoreType.DMA
    V = pltpu.VMEM
    scratch = [
        V((na, 16, BLK), jnp.int32),
        V((na, 16, BLK), jnp.int32),
        V((na, BLK), jnp.int32),
        pltpu.SMEM((na, BLK), jnp.int32),
        V((NO, IBD, BLK, RANK), BF16),
        V((NO, 8, BLK), F32),
        V((NO, IBD, 8, BLK), F32),
        V((NO, IBD, BLK, BLK), F32),
        V((na, BLK, RANK), BF16),
        V((na, BLK, RANK), BF16),
        V((na, BLK, RANK), BF16),
        V((na, BLK, RANK), BF16),
        V((na, QR, RANK), BF16),
        V((na, QR, RANK), BF16),
        V((NO, IBD * BLK, na * BLK), BF16),
        V((NO, HALF, RANK), BF16),
        V((NO, HALF, RANK), BF16),
        V((NO, HALF, RANK), BF16),
        V((NX, ZROWS, RANK), BF16),
        V((NX, HALF, RANK), BF16),
        V((NX, HALF - ZROWS, RANK), BF16),
        V((HALF - ZROWS, RANK), BF16),
        V((HALF - ZROWS, RANK), BF16),
        V((QR, RANK), F32),
        dma((na,)), dma((na,)), dma,
        dma((NX,)), dma((NX,)), dma, dma, dma((NX,)), dma((NX,)), dma((NX,)), dma((NX,)), dma((NO,)), dma((NO,)),
        dma((NX,)), dma((NX,)), dma, dma, dma((NX,)), dma((NX,)),
        dma((na,)), dma((na,)), dma((na,)), dma((na,)),
        dma((na,)), dma((na,)), dma((na,)), dma((na,)),
        dma((na,)), dma((na,)), dma((na,)), dma((na,)),
        dma((NO,)), dma((NO,)), dma((NX,)), dma((NX,)), dma((NX,)), dma((NX,)), dma((NX,)), dma((NX,)), dma, dma,
        dma((2,)), dma((2,)), dma((2,)),
    ]
    vmem = pl.BlockSpec(memory_space=pltpu.VMEM)
    anywhere = pl.BlockSpec(memory_space=pl.ANY)
    new_users, new_items = pl.pallas_call(
        functools.partial(kernel, na),
        out_shape=(
            jax.ShapeDtypeStruct(user_factors.shape, BF16),
            jax.ShapeDtypeStruct((IBD, BLK, RANK), BF16),
        ),
        in_specs=[anywhere, anywhere, vmem, pl.BlockSpec(memory_space=pltpu.SMEM), vmem, vmem],
        out_specs=(vmem, vmem),
        scratch_shapes=scratch,
        compiler_params=pltpu.CompilerParams(
            collective_id=0, has_side_effects=True, vmem_limit_bytes=56 << 20),
    )(
        user_factors,
        item_factors.reshape(IBD, BLK, RANK),
        item_bucket.reshape(IBD, BLK),
        propensity.reshape(1, -1),
        tile_blocks,
        positives.T,
    )
    return new_users, new_items.reshape(item_factors.shape)


def solution(mesh):
    na = mesh.shape["user"] // NX // 2
    return jax.shard_map(
        functools.partial(body, na),
        mesh=mesh,
        in_specs=(
            P("user", None),
            P(("user", "item"), None),
            P(("user", "item")),
            P(),
            P("user", "item"),
            P("user", "item"),
        ),
        out_specs=(P("user", None), P(("user", "item"), None)),
        check_vma=False,
    )
```

```python
import functools

import jax
import jax.numpy as jnp
from jax import lax
from jax.experimental import pallas as pl
from jax.experimental.pallas import tpu as pltpu
from jax.sharding import PartitionSpec as P

BLK = 128
STEP_USER = 0.02
STEP_ITEM = 0.1
DECAY = 0.1
MESH = pl.DeviceIdType.MESH
F32 = jnp.float32
BF16 = jnp.bfloat16

NX = 4
NY = 4
IBD = 6
RANK = 256
HB = IBD // 2
HALF = HB * BLK
QR = BLK // NY
NO = 2 * NX
ZB = 2
ZB2 = 1
ZROWS = ZB2 * BLK
LAG1 = 4
LAG2 = 5


def nt(a, b):
    return lax.dot_general(a, b, (((1,), (1,)), ((), ())), preferred_element_type=F32)


def nn(a, b):
    return lax.dot_general(a, b, (((1,), (0,)), ((), ())), preferred_element_type=F32)


def kernel(na, u_ref, it_ref, bk_ref, prop_ref, tb_ref, pos_ref, ou_ref, oi_ref,
           cm, cr, idv, ids, items, invp, invrow, invcol, ua, ub, gs, yr, zs_buf, zr, slot, prv, lst,
           cs, ccr, xs, zrec, xrec, xrec1, psum, prec, own_sum,
           c_s, c_r, sm_sem, ix_s, ix_r, iz_s, iz_r, jx_s, jx_r, jz_s, jz_r, f_s, f_r,
           p_s, p_r, pz_s, pz_r, pf_s, pf_r,
           az_s, az_r, ay_s, ay_r, ry_s, ry_r, rz_s, rz_r, bz_s, bz_r, by_s, by_r,
           g_s, g_r, x_s, x_r, xb_s, xb_r, w_s, w_r, v_s, v_r, t_s, t_r, o_s, o_r, l_sem):
    user = lax.axis_index("user")
    y = lax.axis_index("item")
    r = lax.axis_index("rep")
    z = user // NX
    x = user % NX
    m = z // 2
    p = z % 2
    own = NX * p
    far = NX - own
    k0 = own + x
    c = RANK ** -0.5

    def zdev(mm):
        return ((2 * mm + p) * NX + x, y, r)

    def xdev(xx):
        return (z * NX + xx, y, r)

    def ydev(yy):
        return (user, yy, r)

    sib = (user, y, 1 - r)
    mate = ((2 * m + 1 - p) * NX + x, y, r)

    def rc(src, dst, ss, rs, dev):
        return pltpu.make_async_remote_copy(
            src_ref=src, dst_ref=dst, send_sem=ss, recv_sem=rs, device_id=dev, device_id_type=MESH)

    def step(i):
        return na // 2 + (2 * (i % 2) - 1) * ((i + 1) // 2)

    def peer(i):
        return lax.rem(m + step(i), na)

    def source(i):
        return lax.rem(m + 2 * na - step(i), na)

    def off(base, i, n):
        return lax.rem(base + i, n)

    barrier = pltpu.get_barrier_semaphore()

    def greet(i, carry):
        pl.semaphore_signal(barrier, inc=1, device_id=zdev(peer(i)), device_id_type=MESH)
        return carry

    lax.fori_loop(0, na - 1, greet, 0)
    for d in range(1, NX):
        pl.semaphore_signal(barrier, inc=1, device_id=xdev(off(x, d, NX)), device_id_type=MESH)
    for d in range(1, NY):
        pl.semaphore_signal(barrier, inc=1, device_id=ydev(off(y, d, NY)), device_id_type=MESH)
    pl.semaphore_signal(barrier, inc=1, device_id=sib, device_id_type=MESH)
    pl.semaphore_signal(barrier, inc=1, device_id=mate, device_id_type=MESH)

    b0 = pl.multiple_of(r * BLK, BLK)
    q0 = pl.multiple_of(y * QR, QR)
    h0 = r * HB
    own_items = pltpu.make_async_copy(it_ref, items.at[k0], l_sem.at[0])
    own_items.start()
    own_users = pltpu.make_async_copy(u_ref.at[pl.ds(b0, BLK)], ua.at[m], l_sem.at[1])
    own_users.start()

    tb = tb_ref[pl.ds(r, 1), :]
    owner = (tb * 2731) >> 16
    local = tb - owner * (NY * IBD) - y * IBD
    ow_rows = lax.broadcasted_iota(jnp.int32, (na * NO, tb.shape[1]), 0)
    hot = jnp.where(ow_rows == owner, 1.0, 0.0)
    pos = pos_ref[:, pl.ds(b0, BLK)].astype(F32).astype(BF16)
    pos_by = nn(hot.astype(BF16), pos)
    named = jnp.sum(hot, axis=1, keepdims=True)
    pos_by = jnp.where(named > 0.0, pos_by, -1.0).astype(jnp.int32)
    m_rows = lax.broadcasted_iota(jnp.int32, (na, tb.shape[1]), 0)
    id_lane = lax.broadcasted_iota(jnp.int32, (na, BLK), 1)
    id_mat = jnp.zeros((na, BLK), jnp.int32)
    for k in range(NO):
        asked = jnp.max(jnp.where(owner == m_rows * NO + k, local + 1, 0), axis=1, keepdims=True)
        id_mat = jnp.where(id_lane == k, asked, id_mat)
    for mm in range(na):
        cm[mm, 0:NO, :] = pos_by[mm * NO:(mm + 1) * NO, :]
        cm[mm, NO:NO + 1, :] = id_mat[mm:mm + 1, :]

    bk = bk_ref[...]
    inv = jnp.zeros((IBD, BLK), F32)
    for b in range(16):
        inv = inv + jnp.where(bk == b, 1.0 / jnp.full((IBD, BLK), prop_ref[0, b], F32), 0.0)
    invp[k0, 0:IBD, :] = inv * (2.0 * c)
    cr[m] = cm[m]

    def code_copy(i):
        mm = peer(i)
        return rc(cm.at[mm], cr.at[m], c_s.at[mm], c_r.at[m], zdev(mm))

    def az_copy(i):
        mm = peer(i)
        part = ua.at[m, pl.ds(q0, QR)]
        return rc(part, part, az_s.at[mm], az_r.at[m], zdev(mm))

    def ix_copy(xx):
        part = items.at[k0, pl.ds(h0, HB)]
        return rc(part, part, ix_s.at[xx], ix_r.at[x], xdev(xx))

    def ix_in(xx):
        part = items.at[own + xx, pl.ds(h0, HB)]
        return rc(part, part, ix_s.at[xx], ix_r.at[xx], xdev(xx))

    def iz_copy(k):
        part = items.at[k, pl.ds(h0, HB)]
        return rc(part, part, iz_s, iz_r, mate)

    def jz_copy(k, xx):
        part = items.at[k, pl.ds(h0 + ZB, HB - ZB)]
        return rc(part, part, jz_s.at[xx], jz_r.at[xx], mate)

    def jx_copy(xx):
        part = items.at[far + x, pl.ds(h0, ZB)]
        return rc(part, part, jx_s.at[xx], jx_r.at[x], xdev(xx))

    def jx_in(xx):
        part = items.at[far + xx, pl.ds(h0, ZB)]
        return rc(part, part, jx_s.at[xx], jx_r.at[xx], xdev(xx))

    def core_items(k, start):
        part = items.at[k, pl.ds(start, HB)]
        return rc(part, part, f_s.at[k], f_r.at[k], sib)

    def p_copy(k, xx, ss, rs, slot):
        return rc(invp.at[k], invp.at[k], ss.at[xx], rs.at[slot], xdev(xx))

    def pz_copy(k):
        return rc(invp.at[k], invp.at[k], pz_s, pz_r, mate)

    own_users.wait()
    own_items.wait()
    pl.semaphore_wait(barrier, na - 1 + NX - 1 + NY - 1 + 2)

    def send_users(i, carry):
        az_copy(i).start()
        return carry

    def send_codes(i, carry):
        code_copy(i).start()
        return carry

    iz_copy(k0).start()
    for d in (1, 3, 2):
        ix_copy(off(x, d, NX)).start()
    lax.fori_loop(0, na - 1, send_users, 0)
    lax.fori_loop(0, na - 1, send_codes, 0)
    for d in (2, 1, 3):
        xx = off(x, d, NX)
        p_copy(k0, xx, p_s, p_r, x).start()
    pz_copy(k0).start()

    def forward_y(buf, mm, ss, rs):
        part = buf.at[mm, pl.ds(q0, QR)]
        for d in (2, 1, 3):
            rc(part, part, ss.at[mm], rs.at[mm], ydev(off(y, d, NY))).start()

    def three(buf, mm, ss, rs):
        part = buf.at[mm, pl.ds(0, QR * (NY - 1))]
        return rc(part, part, ss.at[mm], rs.at[mm], ydev(off(y, 1, NY)))

    def arrive_z(buf, mm, ss, rs):
        part = buf.at[mm, pl.ds(q0, QR)]
        rc(part, part, ss.at[mm], rs.at[mm], zdev(mm)).wait_recv()

    def forward_first(i, carry):
        mm = source(na - 2 - i)
        arrive_z(ua, mm, az_s, az_r)
        forward_y(ua, mm, ay_s, ay_r)
        return carry

    def forward_own(xx):
        ix_in(xx).wait_recv()
        jz_copy(own + xx, xx).start()
        core_items(own + xx, h0).start()

    iz_copy(far + x).wait_recv()
    for d in (2, 1, 3):
        jx_copy(off(x, d, NX)).start()
    core_items(far + x, h0).start()
    lax.fori_loop(0, 2, forward_first, 0)
    forward_own(off(x, 1, NX))
    forward_own(off(x, 3, NX))
    lax.fori_loop(2, 4, forward_first, 0)
    forward_own(off(x, 2, NX))
    pz_copy(far + x).wait_recv()
    for d in (2, 1, 3):
        xx = off(x, d, NX)
        p_copy(far + x, xx, pf_s, pf_r, x).start()
    lax.fori_loop(4, na - 1, forward_first, 0)
    for d in (1, 3, 2):
        xx = off(x, d, NX)
        p_copy(own + xx, xx, p_s, p_r, xx).wait_recv()
        p_copy(far + xx, xx, pf_s, pf_r, xx).wait_recv()

    def take_codes(i, carry):
        mm = source(i)
        rc(cm.at[mm], cr.at[mm], c_s.at[mm], c_r.at[mm], zdev(mm)).wait_recv()
        return carry

    lax.fori_loop(0, na - 1, take_codes, 0)
    for mm in range(na):
        idv[mm:mm + 1, :] = cr[mm, NO:NO + 1, :]
    to_smem = pltpu.make_async_copy(idv, ids, sm_sem)
    to_smem.start()
    for k in range(NO):
        cols = jnp.transpose(invp[k])
        for j in range(IBD):
            invcol[k, j] = jnp.broadcast_to(cols[:, j:j + 1], (BLK, BLK))
            invrow[k, j] = jnp.broadcast_to(invp[k, j:j + 1, :], (8, BLK))
    to_smem.wait()

    def chain(k, carry):
        codes = [ids[source(na - 1 - i), k] for i in range(na)]
        for i in range(na):
            before = 0
            for e in range(i):
                before = jnp.where(codes[e] == codes[i], e + 1, before)
            prv[k, i] = jnp.int32(before)
        for j in range(IBD):
            last = 0
            for i in range(na):
                last = jnp.where(codes[i] == j + 1, i + 1, last)
            lst[k, j] = last
        slot[k, 0] = jnp.zeros((BLK, RANK), F32)
        return carry

    lax.fori_loop(0, NO, chain, 0)
    for d in (1, 3, 2):
        xx = off(x, d, NX)
        jx_in(xx).wait_recv()
        jz_copy(far + xx, xx).wait_recv()
        core_items(far + xx, h0).start()
    o0 = (1 - r) * HB
    core_items(far + x, o0).wait_recv()
    for d in (1, 3, 2):
        xx = off(x, d, NX)
        core_items(own + xx, o0).wait_recv()
        core_items(far + xx, o0).wait_recv()

    lane_f = lax.broadcasted_iota(jnp.int32, (BLK, BLK), 1).astype(F32)
    sub = lax.broadcasted_iota(jnp.int32, (BLK, BLK), 0)

    def pick(mm, k):
        code = ids[mm, k]
        j = jnp.maximum(code - 1, 0)
        flat = jnp.where(code > 0, 2.0 * c, 0.0).astype(F32)
        return code, j, items[k, j], flat

    def grads(mm):
        users = ua[mm]
        cols = jnp.transpose(cr[mm, 0:NO, :].astype(F32))
        total = jnp.zeros((BLK, RANK), F32)
        for part in range(NO // NX):
            picks = [pick(mm, part * NX + q) for q in range(NX)]
            stack = jnp.concatenate([t[2] for t in picks], axis=0)
            scores = nt(users, stack)
            hs = []
            for q in range(NX):
                k = part * NX + q
                code, j, block, flat = picks[q]
                s = scores[:, q * BLK:(q + 1) * BLK]
                hit = cols[:, k:k + 1] == lane_f
                w = invrow[k, j][0:1, :]
                margin = jnp.maximum(1.0 + s * jnp.where(hit, -c, c), 0.0)
                hs.append((margin * jnp.where(hit, -w, flat)).astype(BF16))
            total = total + nn(jnp.concatenate(hs, axis=1), stack)
        return total

    def ry_copy(mm, d):
        yy = off(y, d, NY)
        return rc(gs.at[mm, pl.ds(pl.multiple_of(yy * QR, QR), QR)], yr.at[mm, pl.ds(q0, QR)],
                  ry_s.at[mm], ry_r.at[mm], ydev(yy))

    def rz_copy(mm):
        return rc(zs_buf.at[mm], zr.at[m], rz_s.at[mm], rz_r.at[m], zdev(mm))

    def sum_y(mm):
        part = yr.at[mm, pl.ds(0, QR * (NY - 1))]
        rc(part, part, ry_s.at[mm], ry_r.at[mm], ydev(off(y, 1, NY))).wait_recv()
        total = gs[mm, pl.ds(q0, QR), :].astype(F32)
        for d in range(1, NY):
            total = total + yr[mm, pl.ds(pl.multiple_of(off(y, d, NY) * QR, QR), QR), :].astype(F32)
        return total

    def first_pass(i, carry):
        @pl.when(i < na)
        def _():
            mm = peer(i)

            @pl.when(i < na - 1)
            def _():
                three(ua, mm, ay_s, ay_r).wait_recv()

            gs[mm] = grads(mm).astype(BF16)
            for d in (2, 1, 3):
                ry_copy(mm, d).start()

        @pl.when(i >= LAG1)
        def _():
            mm = peer(i - LAG1)
            total = sum_y(mm)

            @pl.when(i < na - 1 + LAG1)
            def _():
                zs_buf[mm] = total.astype(BF16)
                rz_copy(mm).start()

            @pl.when(i == na - 1 + LAG1)
            def _():
                own_sum[...] = total

        return carry

    lax.fori_loop(0, na + LAG1, first_pass, 0)

    def gather_sum(i, carry):
        mm = source(i)
        rc(zs_buf.at[mm], zr.at[mm], rz_s.at[mm], rz_r.at[mm], zdev(mm)).wait_recv()
        own_sum[...] += zr[mm].astype(F32)
        return carry

    lax.fori_loop(0, na - 1, gather_sum, 0)

    old = ua[m, pl.ds(q0, QR), :].astype(F32)
    ub[m, pl.ds(q0, QR), :] = (old - STEP_USER * (own_sum[...] + DECAY * old)).astype(BF16)

    def bz_copy(i):
        mm = peer(i)
        part = ub.at[m, pl.ds(q0, QR)]
        return rc(part, part, bz_s.at[mm], bz_r.at[m], zdev(mm))

    def send_new(i, carry):
        bz_copy(i).start()
        return carry

    lax.fori_loop(0, na - 1, send_new, 0)
    forward_y(ub, m, by_s, by_r)

    def expand(i, mm):
        users = ub[mm]
        for part in range(NO // NX):
            picks = [pick(mm, part * NX + q) for q in range(NX)]
            scores = nt(jnp.concatenate([t[2] for t in picks], axis=0), users)
            hs = []
            for q in range(NX):
                k = part * NX + q
                code, j, block, flat = picks[q]
                s = scores[q * BLK:(q + 1) * BLK]
                hit = cr[mm, k:k + 1, :] == sub
                margin = jnp.maximum(1.0 + s * jnp.where(hit, -c, c), 0.0)
                hs.append((margin * jnp.where(hit, -invcol[k, j], flat)).astype(BF16))
            terms = nn(jnp.concatenate(hs, axis=0), users)
            for q in range(NX):
                k = part * NX + q
                slot[k, i + 1] = terms[q * BLK:(q + 1) * BLK] + slot[k, prv[k, i]]

    def second_pass(i, carry):
        @pl.when(jnp.logical_and(i > 0, i < na))
        def _():
            mm = source(na - 1 - i)
            arrive_z(ub, mm, bz_s, bz_r)
            forward_y(ub, mm, by_s, by_r)

        @pl.when(i >= LAG2)
        def _():
            mm = source(na - 1 - (i - LAG2))
            three(ub, mm, by_s, by_r).wait_recv()
            expand(i - LAG2, mm)

        return carry

    lax.fori_loop(0, na + LAG2, second_pass, 0)

    ou_ref[pl.ds(b0, BLK), :] = ub[m]
    out_u = rc(ub.at[m], ou_ref.at[pl.ds(b0, BLK)], o_s.at[0], o_r.at[0], sib)
    out_u.start()

    def item_sum(k, b):
        return slot[k, lst[k, b]]

    def core_copy(k):
        return rc(cs.at[k], ccr.at[k], g_s.at[k], g_r.at[k], sib)

    def other_half(k):
        for b in range(HB):
            cs[k, b * BLK:(b + 1) * BLK, :] = item_sum(k, o0 + b).astype(BF16)
        core_copy(k).start()

    def both(k):
        core_copy(k).wait_recv()
        for b in range(HB):
            rows = slice(b * BLK, (b + 1) * BLK)
            xs[k, rows, :] = (item_sum(k, h0 + b) + ccr[k, rows, :].astype(F32)).astype(BF16)

    order = [off(x, d, NX) for d in (2, 1, 3, 0)]
    for xx in order:
        other_half(far + xx)

    def w_copy(xx):
        return rc(xs.at[far + xx, pl.ds(0, ZROWS)], zrec.at[xx], w_s.at[xx], w_r.at[xx], mate)

    def w_in(xx):
        return rc(xs.at[own + xx, pl.ds(0, ZROWS)], zrec.at[xx], w_s.at[xx], w_r.at[xx], mate)

    def v_copy(xx):
        return rc(xs.at[far + xx, pl.ds(ZROWS, HALF - ZROWS)], xrec1.at[x], v_s.at[xx], v_r.at[x], xdev(xx))

    def xa_copy(xx):
        rows = pl.ds(ZROWS, HALF - ZROWS)
        return rc(xs.at[own + xx, rows], xrec.at[x, rows], x_s.at[xx], x_r.at[x], xdev(xx))

    def xb_copy(xx):
        rows = pl.ds(0, ZROWS)
        return rc(xs.at[own + xx, rows], xrec.at[x, rows], xb_s.at[xx], xb_r.at[x], xdev(xx))

    for n, xx in enumerate(order):
        other_half(own + xx)
        both(far + xx)
        w_copy(xx).start()
        if n < NX - 1:
            v_copy(xx).start()

    for n, xx in enumerate(order):
        both(own + xx)
        if n < NX - 1:
            xa_copy(xx).start()

    for n, xx in enumerate(order):
        k = own + xx
        w_in(xx).wait_recv()
        rows = pl.ds(0, ZROWS)
        xs[k, rows, :] = (xs[k, rows, :].astype(F32) + zrec[xx].astype(F32)).astype(BF16)
        if n < NX - 1:
            xb_copy(xx).start()

    part = xs[far + x, pl.ds(ZROWS, HALF - ZROWS), :].astype(F32)
    for d in (1, 3, 2):
        xx = off(x, d, NX)
        rc(xrec1.at[xx], xrec1.at[xx], v_s.at[xx], v_r.at[xx], xdev(xx)).wait_recv()
        part = part + xrec1[xx].astype(F32)
    psum[...] = part.astype(BF16)
    to_mate = rc(psum, prec, t_s, t_r, mate)
    to_mate.start()

    for d in (1, 3, 2):
        xx = off(x, d, NX)
        lower, upper = xrec.at[xx, pl.ds(0, ZROWS)], xrec.at[xx, pl.ds(ZROWS, HALF - ZROWS)]
        rc(upper, upper, x_s.at[xx], x_r.at[xx], xdev(xx)).wait_recv()
        rc(lower, lower, xb_s.at[xx], xb_r.at[xx], xdev(xx)).wait_recv()
    to_mate.wait_recv()
    for b in range(HB):
        rows = pl.ds(b * BLK, BLK)
        total = xs[k0, rows, :].astype(F32)
        for d in range(1, NX):
            total = total + xrec[off(x, d, NX), rows, :].astype(F32)
        if b >= ZB2:
            total = total + prec[pl.ds((b - ZB2) * BLK, BLK), :].astype(F32)
        olds = items[k0, h0 + b].astype(F32)
        oi_ref[h0 + b] = (olds - STEP_ITEM * (total + DECAY * olds)).astype(BF16)
    mine = oi_ref.at[pl.ds(h0, HB)]
    out_i = rc(mine, mine, o_s.at[1], o_r.at[1], sib)
    out_i.start()

    iz_copy(k0).wait_send()
    pz_copy(k0).wait_send()
    to_mate.wait_send()
    core_items(far + x, h0).wait_send()
    for d in range(NX):
        xx = off(x, d, NX)
        core_copy(own + xx).wait_send()
        core_copy(far + xx).wait_send()
        w_copy(xx).wait_send()
        if d:
            ix_copy(xx).wait_send()
            jx_copy(xx).wait_send()
            jz_copy(own + xx, xx).wait_send()
            core_items(own + xx, h0).wait_send()
            core_items(far + xx, h0).wait_send()
            p_copy(k0, xx, p_s, p_r, x).wait_send()
            p_copy(far + x, xx, pf_s, pf_r, x).wait_send()
            v_copy(xx).wait_send()
            xa_copy(xx).wait_send()
            xb_copy(xx).wait_send()

    def sent(i, carry):
        code_copy(i).wait_send()
        az_copy(i).wait_send()
        bz_copy(i).wait_send()
        mm = peer(i)
        three(ua, mm, ay_s, ay_r).wait_send()
        rz_copy(mm).wait_send()
        return carry

    lax.fori_loop(0, na - 1, sent, 0)

    def sent_all(i, carry):
        three(ub, i, by_s, by_r).wait_send()
        three(gs, i, ry_s, ry_r).wait_send()
        return carry

    lax.fori_loop(0, na, sent_all, 0)
    out_u.wait_send()
    out_i.wait_send()
    other_b = pl.multiple_of((1 - r) * BLK, BLK)
    rc(ub.at[m], ou_ref.at[pl.ds(other_b, BLK)], o_s.at[0], o_r.at[0], sib).wait_recv()
    theirs = oi_ref.at[pl.ds(o0, HB)]
    rc(theirs, theirs, o_s.at[1], o_r.at[1], sib).wait_recv()


def body(na, user_factors, item_factors, item_bucket, propensity, tile_blocks, positives):
    dma = pltpu.SemaphoreType.DMA
    V = pltpu.VMEM
    scratch = [
        V((na, 16, BLK), jnp.int32),
        V((na, 16, BLK), jnp.int32),
        V((na, BLK), jnp.int32),
        pltpu.SMEM((na, BLK), jnp.int32),
        V((NO, IBD, BLK, RANK), BF16),
        V((NO, 8, BLK), F32),
        V((NO, IBD, 8, BLK), F32),
        V((NO, IBD, BLK, BLK), F32),
        V((na, BLK, RANK), BF16),
        V((na, BLK, RANK), BF16),
        V((na, BLK, RANK), BF16),
        V((na, BLK, RANK), BF16),
        V((na, QR, RANK), BF16),
        V((na, QR, RANK), BF16),
        V((NO, na + 1, BLK, RANK), F32),
        pltpu.SMEM((NO, na), jnp.int32),
        pltpu.SMEM((NO, IBD), jnp.int32),
        V((NO, HALF, RANK), BF16),
        V((NO, HALF, RANK), BF16),
        V((NO, HALF, RANK), BF16),
        V((NX, ZROWS, RANK), BF16),
        V((NX, HALF, RANK), BF16),
        V((NX, HALF - ZROWS, RANK), BF16),
        V((HALF - ZROWS, RANK), BF16),
        V((HALF - ZROWS, RANK), BF16),
        V((QR, RANK), F32),
        dma((na,)), dma((na,)), dma,
        dma((NX,)), dma((NX,)), dma, dma, dma((NX,)), dma((NX,)), dma((NX,)), dma((NX,)), dma((NO,)), dma((NO,)),
        dma((NX,)), dma((NX,)), dma, dma, dma((NX,)), dma((NX,)),
        dma((na,)), dma((na,)), dma((na,)), dma((na,)),
        dma((na,)), dma((na,)), dma((na,)), dma((na,)),
        dma((na,)), dma((na,)), dma((na,)), dma((na,)),
        dma((NO,)), dma((NO,)), dma((NX,)), dma((NX,)), dma((NX,)), dma((NX,)),
        dma((NX,)), dma((NX,)), dma((NX,)), dma((NX,)), dma, dma,
        dma((2,)), dma((2,)), dma((2,)),
    ]
    vmem = pl.BlockSpec(memory_space=pltpu.VMEM)
    anywhere = pl.BlockSpec(memory_space=pl.ANY)
    new_users, new_items = pl.pallas_call(
        functools.partial(kernel, na),
        out_shape=(
            jax.ShapeDtypeStruct(user_factors.shape, BF16),
            jax.ShapeDtypeStruct((IBD, BLK, RANK), BF16),
        ),
        in_specs=[anywhere, anywhere, vmem, pl.BlockSpec(memory_space=pltpu.SMEM), vmem, vmem],
        out_specs=(vmem, vmem),
        scratch_shapes=scratch,
        compiler_params=pltpu.CompilerParams(
            collective_id=0, has_side_effects=True, vmem_limit_bytes=56 << 20),
    )(
        user_factors,
        item_factors.reshape(IBD, BLK, RANK),
        item_bucket.reshape(IBD, BLK),
        propensity.reshape(1, -1),
        tile_blocks,
        positives.T,
    )
    return new_users, new_items.reshape(item_factors.shape)


def solution(mesh):
    na = mesh.shape["user"] // NX // 2
    return jax.shard_map(
        functools.partial(body, na),
        mesh=mesh,
        in_specs=(
            P("user", None),
            P(("user", "item"), None),
            P(("user", "item")),
            P(),
            P("user", "item"),
            P("user", "item"),
        ),
        out_specs=(P("user", None), P(("user", "item"), None)),
        check_vma=False,
    )
```

```python
import functools

import jax
import jax.numpy as jnp
from jax import lax
from jax.experimental import pallas as pl
from jax.experimental.pallas import tpu as pltpu
from jax.sharding import PartitionSpec as P

BLK = 128
STEP_USER = 0.02
STEP_ITEM = 0.1
DECAY = 0.1
MESH = pl.DeviceIdType.MESH
F32 = jnp.float32
BF16 = jnp.bfloat16

NX = 4
NY = 4
IBD = 6
RANK = 256
HB = IBD // 2
HALF = HB * BLK
QR = BLK // NY
NO = 2 * NX
ZB = 2
ZROWS = 3 * BLK // 2
CUT = BLK // 2
LAG1 = 4
LAG2 = 5


def nt(a, b):
    return lax.dot_general(a, b, (((1,), (1,)), ((), ())), preferred_element_type=F32)


def nn(a, b):
    return lax.dot_general(a, b, (((1,), (0,)), ((), ())), preferred_element_type=F32)


def kernel(na, u_ref, it_ref, bk_in, prop_in, tb_in, pos_in, ou_ref, oi_ref,
           bk_ref, prop_ref, tb_ref, pos_ref,
           cm, cr, idv, ids, items, invp, invrow, invcol, ua, ub, gs, yr, zs_buf, zr, slot, prv, lst,
           cs, ccr, xs, zrec, xrec, xrec1, psum, prec, own_sum, fin,
           c_s, c_r, sm_sem, ix_s, ix_r, iz_s, iz_r, jx_s, jx_r, jz_s, jz_r, f_s, f_r, e_s, e_r,
           p_s, p_r, pz_s, pz_r, pf_s, pf_r,
           az_s, az_r, ay_s, ay_r, ry_s, ry_r, rz_s, rz_r, bz_s, bz_r, by_s, by_r,
           g_s, g_r, x_s, x_r, xb_s, xb_r, w_s, w_r, v_s, v_r, t_s, t_r, o_s, o_r, l_sem):
    user = lax.axis_index("user")
    y = lax.axis_index("item")
    r = lax.axis_index("rep")
    z = user // NX
    x = user % NX
    m = z // 2
    p = z % 2
    own = NX * p
    far = NX - own
    k0 = own + x
    c = RANK ** -0.5

    def zdev(mm):
        return ((2 * mm + p) * NX + x, y, r)

    def xdev(xx):
        return (z * NX + xx, y, r)

    def ydev(yy):
        return (user, yy, r)

    sib = (user, y, 1 - r)
    mate = ((2 * m + 1 - p) * NX + x, y, r)

    def rc(src, dst, ss, rs, dev):
        return pltpu.make_async_remote_copy(
            src_ref=src, dst_ref=dst, send_sem=ss, recv_sem=rs, device_id=dev, device_id_type=MESH)

    def step(i):
        return na // 2 + (2 * (i % 2) - 1) * ((i + 1) // 2)

    def peer(i):
        return lax.rem(m + step(i), na)

    def source(i):
        return lax.rem(m + 2 * na - step(i), na)

    def off(base, i, n):
        return lax.rem(base + i, n)

    barrier = pltpu.get_barrier_semaphore()

    def greet(i, carry):
        pl.semaphore_signal(barrier, inc=1, device_id=zdev(peer(i)), device_id_type=MESH)
        return carry

    lax.fori_loop(0, na - 1, greet, 0)
    for d in range(1, NX):
        pl.semaphore_signal(barrier, inc=1, device_id=xdev(off(x, d, NX)), device_id_type=MESH)
    for d in range(1, NY):
        pl.semaphore_signal(barrier, inc=1, device_id=ydev(off(y, d, NY)), device_id_type=MESH)
    pl.semaphore_signal(barrier, inc=1, device_id=sib, device_id_type=MESH)
    pl.semaphore_signal(barrier, inc=1, device_id=mate, device_id_type=MESH)

    b0 = pl.multiple_of(r * BLK, BLK)
    q0 = pl.multiple_of(y * QR, QR)
    h0 = r * HB
    own_items = pltpu.make_async_copy(it_ref, items.at[k0], l_sem.at[0])
    own_items.start()
    own_users = pltpu.make_async_copy(u_ref.at[pl.ds(b0, BLK)], ua.at[m], l_sem.at[1])
    own_users.start()

    small = [pltpu.make_async_copy(a, b, l_sem.at[2 + n]) for n, (a, b) in enumerate(
        ((tb_in, tb_ref), (pos_in, pos_ref), (bk_in, bk_ref), (prop_in, prop_ref)))]
    for copy in small:
        copy.start()
    for copy in small:
        copy.wait()

    tb = tb_ref[pl.ds(r, 1), :]
    owner = (tb * 2731) >> 16
    local = tb - owner * (NY * IBD) - y * IBD
    ow_rows = lax.broadcasted_iota(jnp.int32, (na * NO, tb.shape[1]), 0)
    hot = jnp.where(ow_rows == owner, 1.0, 0.0)
    pos = pos_ref[:, pl.ds(b0, BLK)].astype(F32).astype(BF16)
    pos_by = nn(hot.astype(BF16), pos)
    named = jnp.sum(hot, axis=1, keepdims=True)
    pos_by = jnp.where(named > 0.0, pos_by, -1.0).astype(jnp.int32)
    m_rows = lax.broadcasted_iota(jnp.int32, (na, tb.shape[1]), 0)
    id_lane = lax.broadcasted_iota(jnp.int32, (na, BLK), 1)
    id_mat = jnp.zeros((na, BLK), jnp.int32)
    for k in range(NO):
        asked = jnp.max(jnp.where(owner == m_rows * NO + k, local + 1, 0), axis=1, keepdims=True)
        id_mat = jnp.where(id_lane == k, asked, id_mat)
    for mm in range(na):
        cm[mm, 0:NO, :] = pos_by[mm * NO:(mm + 1) * NO, :]
        cm[mm, NO:NO + 1, :] = id_mat[mm:mm + 1, :]

    bk = bk_ref[...]
    inv = jnp.zeros((IBD, BLK), F32)
    for b in range(16):
        inv = inv + jnp.where(bk == b, 1.0 / jnp.full((IBD, BLK), prop_ref[0, b], F32), 0.0)
    invp[k0, 0:IBD, :] = inv * (2.0 * c)
    cr[m] = cm[m]

    def code_copy(i):
        mm = peer(i)
        return rc(cm.at[mm], cr.at[m], c_s.at[mm], c_r.at[m], zdev(mm))

    def az_copy(i):
        mm = peer(i)
        part = ua.at[m, pl.ds(q0, QR)]
        return rc(part, part, az_s.at[mm], az_r.at[m], zdev(mm))

    def ix_copy(xx):
        part = items.at[k0, pl.ds(h0, HB)]
        return rc(part, part, ix_s.at[xx], ix_r.at[x], xdev(xx))

    def ix_in(xx):
        part = items.at[own + xx, pl.ds(h0, HB)]
        return rc(part, part, ix_s.at[xx], ix_r.at[xx], xdev(xx))

    def iz_copy(k):
        part = items.at[k, pl.ds(h0, HB)]
        return rc(part, part, iz_s, iz_r, mate)

    def jz_copy(k, xx):
        part = items.at[k, pl.ds(h0 + ZB, HB - ZB)]
        return rc(part, part, jz_s.at[xx], jz_r.at[xx], mate)

    def jx_copy(xx):
        part = items.at[far + x, pl.ds(h0, ZB)]
        return rc(part, part, jx_s.at[xx], jx_r.at[x], xdev(xx))

    def jx_in(xx):
        part = items.at[far + xx, pl.ds(h0, ZB)]
        return rc(part, part, jx_s.at[xx], jx_r.at[xx], xdev(xx))

    def core_items(k, start):
        part = items.at[k, pl.ds(start, HB)]
        return rc(part, part, f_s.at[k], f_r.at[k], sib)

    def core_part(k, start, count, ss, rs):
        part = items.at[k, pl.ds(start, count)]
        return rc(part, part, ss, rs, sib)

    def core_far(xx, start, last):
        if last:
            return core_part(far + xx, start + ZB, HB - ZB, e_s.at[xx], e_r.at[xx])
        return core_part(far + xx, start, ZB, f_s.at[far + xx], f_r.at[far + xx])

    def p_copy(k, xx, ss, rs, slot):
        return rc(invp.at[k], invp.at[k], ss.at[xx], rs.at[slot], xdev(xx))

    def pz_copy(k):
        return rc(invp.at[k], invp.at[k], pz_s, pz_r, mate)

    own_users.wait()
    own_items.wait()
    pl.semaphore_wait(barrier, na - 1 + NX - 1 + NY - 1 + 2)

    def send_users(i, carry):
        az_copy(i).start()
        return carry

    def send_codes(i, carry):
        code_copy(i).start()
        return carry

    iz_copy(k0).start()
    for d in (1, 3, 2):
        ix_copy(off(x, d, NX)).start()
    lax.fori_loop(0, na - 1, send_users, 0)
    lax.fori_loop(0, na - 1, send_codes, 0)
    for d in (2, 1, 3):
        xx = off(x, d, NX)
        p_copy(k0, xx, p_s, p_r, x).start()
    pz_copy(k0).start()

    def forward_y(buf, mm, ss, rs):
        part = buf.at[mm, pl.ds(q0, QR)]
        for d in (2, 1, 3):
            rc(part, part, ss.at[mm], rs.at[mm], ydev(off(y, d, NY))).start()

    def three(buf, mm, ss, rs):
        part = buf.at[mm, pl.ds(0, QR * (NY - 1))]
        return rc(part, part, ss.at[mm], rs.at[mm], ydev(off(y, 1, NY)))

    def arrive_z(buf, mm, ss, rs):
        part = buf.at[mm, pl.ds(q0, QR)]
        rc(part, part, ss.at[mm], rs.at[mm], zdev(mm)).wait_recv()

    def forward_first(i, carry):
        mm = source(na - 2 - i)
        arrive_z(ua, mm, az_s, az_r)
        forward_y(ua, mm, ay_s, ay_r)
        return carry

    def forward_own(xx):
        ix_in(xx).wait_recv()
        jz_copy(own + xx, xx).start()
        core_items(own + xx, h0).start()

    iz_copy(far + x).wait_recv()
    for d in (2, 1, 3):
        jx_copy(off(x, d, NX)).start()
    core_items(far + x, h0).start()
    lax.fori_loop(0, 2, forward_first, 0)
    forward_own(off(x, 1, NX))
    forward_own(off(x, 3, NX))
    lax.fori_loop(2, 4, forward_first, 0)
    forward_own(off(x, 2, NX))
    pz_copy(far + x).wait_recv()
    for d in (2, 1, 3):
        xx = off(x, d, NX)
        p_copy(far + x, xx, pf_s, pf_r, x).start()
    lax.fori_loop(4, na - 1, forward_first, 0)
    for d in (1, 3, 2):
        xx = off(x, d, NX)
        p_copy(own + xx, xx, p_s, p_r, xx).wait_recv()
        p_copy(far + xx, xx, pf_s, pf_r, xx).wait_recv()

    def take_codes(i, carry):
        mm = source(i)
        rc(cm.at[mm], cr.at[mm], c_s.at[mm], c_r.at[mm], zdev(mm)).wait_recv()
        return carry

    lax.fori_loop(0, na - 1, take_codes, 0)
    for mm in range(na):
        idv[mm:mm + 1, :] = cr[mm, NO:NO + 1, :]
    to_smem = pltpu.make_async_copy(idv, ids, sm_sem)
    to_smem.start()
    for k in range(NO):
        for j in range(IBD):
            invrow[k, j] = jnp.broadcast_to(invp[k, j:j + 1, :], (8, BLK))
    to_smem.wait()

    for d in (1, 3, 2):
        xx = off(x, d, NX)
        jz_copy(far + xx, xx).wait_recv()
        core_far(xx, h0, True).start()
    for d in (1, 3, 2):
        xx = off(x, d, NX)
        jx_in(xx).wait_recv()
        core_far(xx, h0, False).start()
    o0 = (1 - r) * HB
    core_items(far + x, o0).wait_recv()
    for d in (1, 3, 2):
        xx = off(x, d, NX)
        core_items(own + xx, o0).wait_recv()
        core_far(xx, o0, True).wait_recv()
        core_far(xx, o0, False).wait_recv()

    lane_f = lax.broadcasted_iota(jnp.int32, (BLK, BLK), 1).astype(F32)
    sub = lax.broadcasted_iota(jnp.int32, (BLK, BLK), 0)

    def pick(mm, k):
        code = ids[mm, k]
        j = jnp.maximum(code - 1, 0)
        flat = jnp.where(code > 0, 2.0 * c, 0.0).astype(F32)
        return code, j, items[k, j], flat

    def grads(mm):
        users = ua[mm]
        cols = jnp.transpose(cr[mm, 0:NO, :].astype(F32))
        total = jnp.zeros((BLK, RANK), F32)
        for part in range(NO // NX):
            picks = [pick(mm, part * NX + q) for q in range(NX)]
            stack = jnp.concatenate([t[2] for t in picks], axis=0)
            scores = nt(users, stack)
            hs = []
            for q in range(NX):
                k = part * NX + q
                code, j, block, flat = picks[q]
                s = scores[:, q * BLK:(q + 1) * BLK]
                hit = cols[:, k:k + 1] == lane_f
                w = invrow[k, j][0:1, :]
                margin = jnp.maximum(1.0 + s * jnp.where(hit, -c, c), 0.0)
                hs.append((margin * jnp.where(hit, -w, flat)).astype(BF16))
            total = total + nn(jnp.concatenate(hs, axis=1), stack)
        return total

    def ry_copy(mm, d):
        yy = off(y, d, NY)
        return rc(gs.at[mm, pl.ds(pl.multiple_of(yy * QR, QR), QR)], yr.at[mm, pl.ds(q0, QR)],
                  ry_s.at[mm], ry_r.at[mm], ydev(yy))

    def rz_copy(mm):
        return rc(zs_buf.at[mm], zr.at[m], rz_s.at[mm], rz_r.at[m], zdev(mm))

    def sum_y(mm):
        part = yr.at[mm, pl.ds(0, QR * (NY - 1))]
        rc(part, part, ry_s.at[mm], ry_r.at[mm], ydev(off(y, 1, NY))).wait_recv()
        total = gs[mm, pl.ds(q0, QR), :].astype(F32)
        for d in range(1, NY):
            total = total + yr[mm, pl.ds(pl.multiple_of(off(y, d, NY) * QR, QR), QR), :].astype(F32)
        return total

    def first_pass(i, carry):
        @pl.when(i < na)
        def _():
            mm = peer(i)

            @pl.when(i < na - 1)
            def _():
                three(ua, mm, ay_s, ay_r).wait_recv()

            gs[mm] = grads(mm).astype(BF16)
            for d in (2, 1, 3):
                ry_copy(mm, d).start()

        @pl.when(i >= LAG1)
        def _():
            mm = peer(i - LAG1)
            total = sum_y(mm)

            @pl.when(i < na - 1 + LAG1)
            def _():
                zs_buf[mm] = total.astype(BF16)
                rz_copy(mm).start()

            @pl.when(i == na - 1 + LAG1)
            def _():
                own_sum[...] = total

        return carry

    lax.fori_loop(0, na + LAG1, first_pass, 0)

    def chain(k, carry):
        codes = [ids[source(na - 1 - i), k] for i in range(na)]
        for i in range(na):
            before = 0
            for e in range(i):
                before = jnp.where(codes[e] == codes[i], e + 1, before)
            prv[k, i] = jnp.int32(before)
        for j in range(IBD):
            last = 0
            for i in range(na):
                last = jnp.where(codes[i] == j + 1, i + 1, last)
            lst[k, j] = last
        cols = jnp.transpose(invp[k])
        for j in range(IBD):
            invcol[k, j] = jnp.broadcast_to(cols[:, j:j + 1], (BLK, BLK))
        slot[k, 0] = jnp.zeros((BLK, RANK), F32)
        return carry

    lax.fori_loop(0, NO, chain, 0)

    def gather_sum(i, carry):
        mm = source(i)
        rc(zs_buf.at[mm], zr.at[mm], rz_s.at[mm], rz_r.at[mm], zdev(mm)).wait_recv()
        own_sum[...] += zr[mm].astype(F32)
        return carry

    lax.fori_loop(0, na - 1, gather_sum, 0)

    old = ua[m, pl.ds(q0, QR), :].astype(F32)
    ub[m, pl.ds(q0, QR), :] = (old - STEP_USER * (own_sum[...] + DECAY * old)).astype(BF16)

    def bz_copy(i):
        mm = peer(i)
        part = ub.at[m, pl.ds(q0, QR)]
        return rc(part, part, bz_s.at[mm], bz_r.at[m], zdev(mm))

    def send_new(i, carry):
        bz_copy(na - 2 - i).start()
        return carry

    lax.fori_loop(0, na - 1, send_new, 0)
    forward_y(ub, m, by_s, by_r)

    def expand(i, mm):
        users = ub[mm]
        for part in range(NO // NX):
            picks = [pick(mm, part * NX + q) for q in range(NX)]
            scores = nt(jnp.concatenate([t[2] for t in picks], axis=0), users)
            hs = []
            for q in range(NX):
                k = part * NX + q
                code, j, block, flat = picks[q]
                s = scores[q * BLK:(q + 1) * BLK]
                hit = cr[mm, k:k + 1, :] == sub
                margin = jnp.maximum(1.0 + s * jnp.where(hit, -c, c), 0.0)
                hs.append((margin * jnp.where(hit, -invcol[k, j], flat)).astype(BF16))
            terms = nn(jnp.concatenate(hs, axis=0), users)
            for q in range(NX):
                k = part * NX + q
                slot[k, i + 1] = terms[q * BLK:(q + 1) * BLK] + slot[k, prv[k, i]]

    def second_pass(i, carry):
        @pl.when(jnp.logical_and(i > 0, i < na))
        def _():
            mm = source(na - 1 - i)
            arrive_z(ub, mm, bz_s, bz_r)
            forward_y(ub, mm, by_s, by_r)

        @pl.when(i >= LAG2)
        def _():
            mm = source(na - 1 - (i - LAG2))
            three(ub, mm, by_s, by_r).wait_recv()
            expand(i - LAG2, mm)

        return carry

    lax.fori_loop(0, na + LAG2, second_pass, 0)

    keep_u = pltpu.make_async_copy(ub.at[m], ou_ref.at[pl.ds(b0, BLK)], l_sem.at[0])
    keep_u.start()
    out_u = rc(ub.at[m], ou_ref.at[pl.ds(b0, BLK)], o_s.at[0], o_r.at[0], sib)
    out_u.start()

    def item_sum(k, b):
        return slot[k, lst[k, b]]

    def core_copy(k):
        return rc(cs.at[k], ccr.at[k], g_s.at[k], g_r.at[k], sib)

    def other_half(k):
        for b in range(HB):
            cs[k, b * BLK:(b + 1) * BLK, :] = item_sum(k, o0 + b).astype(BF16)
        core_copy(k).start()

    def both(k):
        core_copy(k).wait_recv()
        for b in range(HB):
            rows = slice(b * BLK, (b + 1) * BLK)
            xs[k, rows, :] = (item_sum(k, h0 + b) + ccr[k, rows, :].astype(F32)).astype(BF16)

    def w_copy(xx):
        return rc(xs.at[far + xx, pl.ds(0, ZROWS)], zrec.at[xx], w_s.at[xx], w_r.at[xx], mate)

    def w_in(xx):
        return rc(xs.at[own + xx, pl.ds(0, ZROWS)], zrec.at[xx], w_s.at[xx], w_r.at[xx], mate)

    def v_copy(xx):
        return rc(xs.at[far + xx, pl.ds(ZROWS, HALF - ZROWS)], xrec1.at[x], v_s.at[xx], v_r.at[x], xdev(xx))

    def xa_copy(xx):
        rows = pl.ds(ZROWS, HALF - ZROWS)
        return rc(xs.at[own + xx, rows], xrec.at[x, rows], x_s.at[xx], x_r.at[x], xdev(xx))

    def xb_copy(xx):
        rows = pl.ds(0, ZROWS)
        return rc(xs.at[own + xx, rows], xrec.at[x, rows], xb_s.at[xx], xb_r.at[x], xdev(xx))

    order = [off(x, d, NX) for d in (2, 1, 3, 0)]
    owners = [far + xx for xx in order] + [own + xx for xx in order]
    other_half(owners[0])
    other_half(owners[1])
    for n, k in enumerate(owners):
        if n + 2 < NO:
            other_half(owners[n + 2])
        both(k)
        xx = order[n % NX]
        if n < NX:
            w_copy(xx).start()
            if n < NX - 1:
                v_copy(xx).start()
        elif n < NO - 1:
            xa_copy(xx).start()

    for n, xx in enumerate(order):
        k = own + xx
        w_in(xx).wait_recv()
        rows = pl.ds(0, ZROWS)
        xs[k, rows, :] = (xs[k, rows, :].astype(F32) + zrec[xx].astype(F32)).astype(BF16)
        if n < NX - 1:
            xb_copy(xx).start()

    part = xs[far + x, pl.ds(ZROWS, HALF - ZROWS), :].astype(F32)
    for d in (1, 3, 2):
        xx = off(x, d, NX)
        rc(xrec1.at[xx], xrec1.at[xx], v_s.at[xx], v_r.at[xx], xdev(xx)).wait_recv()
        part = part + xrec1[xx].astype(F32)
    psum[...] = part.astype(BF16)
    to_mate = rc(psum, prec, t_s, t_r, mate)
    to_mate.start()

    for d in (1, 3, 2):
        xx = off(x, d, NX)
        lower, upper = xrec.at[xx, pl.ds(0, ZROWS)], xrec.at[xx, pl.ds(ZROWS, HALF - ZROWS)]
        rc(upper, upper, x_s.at[xx], x_r.at[xx], xdev(xx)).wait_recv()
        rc(lower, lower, xb_s.at[xx], xb_r.at[xx], xdev(xx)).wait_recv()
    to_mate.wait_recv()
    def out_item(b, start):
        return rc(fin.at[b], oi_ref.at[start + b], o_s.at[1 + b], o_r.at[1 + b], sib)

    def keep_item(b):
        return pltpu.make_async_copy(fin.at[b], oi_ref.at[h0 + b], l_sem.at[1 + b])

    for b in range(2 * HB):
        rows = pl.ds(b * CUT, CUT)
        total = xs[k0, rows, :].astype(F32)
        for d in range(1, NX):
            total = total + xrec[off(x, d, NX), rows, :].astype(F32)
        if b * CUT >= ZROWS:
            total = total + prec[pl.ds(b * CUT - ZROWS, CUT), :].astype(F32)
        piece = pl.ds(b % 2 * CUT, CUT)
        olds = items[k0, h0 + b // 2, piece, :].astype(F32)
        fin[b // 2, piece, :] = (olds - STEP_ITEM * (total + DECAY * olds)).astype(BF16)
        if b % 2:
            out_item(b // 2, h0).start()
            keep_item(b // 2).start()

    iz_copy(k0).wait_send()
    pz_copy(k0).wait_send()
    to_mate.wait_send()
    core_items(far + x, h0).wait_send()
    for d in range(NX):
        xx = off(x, d, NX)
        core_copy(own + xx).wait_send()
        core_copy(far + xx).wait_send()
        w_copy(xx).wait_send()
        if d:
            ix_copy(xx).wait_send()
            jx_copy(xx).wait_send()
            jz_copy(own + xx, xx).wait_send()
            core_items(own + xx, h0).wait_send()
            core_far(xx, h0, True).wait_send()
            core_far(xx, h0, False).wait_send()
            p_copy(k0, xx, p_s, p_r, x).wait_send()
            p_copy(far + x, xx, pf_s, pf_r, x).wait_send()
            v_copy(xx).wait_send()
            xa_copy(xx).wait_send()
            xb_copy(xx).wait_send()

    def sent(i, carry):
        code_copy(i).wait_send()
        az_copy(i).wait_send()
        bz_copy(i).wait_send()
        mm = peer(i)
        three(ua, mm, ay_s, ay_r).wait_send()
        rz_copy(mm).wait_send()
        return carry

    lax.fori_loop(0, na - 1, sent, 0)

    def sent_all(i, carry):
        three(ub, i, by_s, by_r).wait_send()
        three(gs, i, ry_s, ry_r).wait_send()
        return carry

    lax.fori_loop(0, na, sent_all, 0)
    out_u.wait_send()
    keep_u.wait()
    other_b = pl.multiple_of((1 - r) * BLK, BLK)
    rc(ub.at[m], ou_ref.at[pl.ds(other_b, BLK)], o_s.at[0], o_r.at[0], sib).wait_recv()
    for b in range(HB):
        keep_item(b).wait()
        out_item(b, h0).wait_send()
        out_item(b, o0).wait_recv()


def hand_over(u_ref, i_ref, ou_ref, oi_ref):
    ou_ref[...] = u_ref[...]
    oi_ref[...] = i_ref[...]


def body(na, user_factors, item_factors, item_bucket, propensity, tile_blocks, positives):
    dma = pltpu.SemaphoreType.DMA
    V = pltpu.VMEM
    scratch = [
        V((IBD, BLK), jnp.int32),
        pltpu.SMEM((1, propensity.shape[0]), F32),
        V(tile_blocks.shape, jnp.int32),
        V((positives.shape[1], positives.shape[0]), jnp.int32),
        V((na, 16, BLK), jnp.int32),
        V((na, 16, BLK), jnp.int32),
        V((na, BLK), jnp.int32),
        pltpu.SMEM((na, BLK), jnp.int32),
        V((NO, IBD, BLK, RANK), BF16),
        V((NO, 8, BLK), F32),
        V((NO, IBD, 8, BLK), F32),
        V((NO, IBD, BLK, BLK), F32),
        V((na, BLK, RANK), BF16),
        V((na, BLK, RANK), BF16),
        V((na, BLK, RANK), BF16),
        V((na, BLK, RANK), BF16),
        V((na, QR, RANK), BF16),
        V((na, QR, RANK), BF16),
        V((NO, na + 1, BLK, RANK), F32),
        pltpu.SMEM((NO, na), jnp.int32),
        pltpu.SMEM((NO, IBD), jnp.int32),
        V((NO, HALF, RANK), BF16),
        V((NO, HALF, RANK), BF16),
        V((NO, HALF, RANK), BF16),
        V((NX, ZROWS, RANK), BF16),
        V((NX, HALF, RANK), BF16),
        V((NX, HALF - ZROWS, RANK), BF16),
        V((HALF - ZROWS, RANK), BF16),
        V((HALF - ZROWS, RANK), BF16),
        V((QR, RANK), F32),
        V((HB, BLK, RANK), BF16),
        dma((na,)), dma((na,)), dma,
        dma((NX,)), dma((NX,)), dma, dma, dma((NX,)), dma((NX,)), dma((NX,)), dma((NX,)), dma((NO,)), dma((NO,)),
        dma((NX,)), dma((NX,)),
        dma((NX,)), dma((NX,)), dma, dma, dma((NX,)), dma((NX,)),
        dma((na,)), dma((na,)), dma((na,)), dma((na,)),
        dma((na,)), dma((na,)), dma((na,)), dma((na,)),
        dma((na,)), dma((na,)), dma((na,)), dma((na,)),
        dma((NO,)), dma((NO,)), dma((NX,)), dma((NX,)), dma((NX,)), dma((NX,)),
        dma((NX,)), dma((NX,)), dma((NX,)), dma((NX,)), dma, dma,
        dma((1 + HB,)), dma((1 + HB,)), dma((6,)),
    ]
    vmem = pl.BlockSpec(memory_space=pltpu.VMEM)
    anywhere = pl.BlockSpec(memory_space=pl.ANY)
    new_users, new_items = pl.pallas_call(
        functools.partial(kernel, na),
        out_shape=(
            jax.ShapeDtypeStruct(user_factors.shape, BF16),
            jax.ShapeDtypeStruct((IBD, BLK, RANK), BF16),
        ),
        in_specs=[anywhere] * 6,
        out_specs=(anywhere, anywhere),
        scratch_shapes=scratch,
        compiler_params=pltpu.CompilerParams(
            collective_id=0, has_side_effects=True, vmem_limit_bytes=56 << 20),
    )(
        user_factors,
        item_factors.reshape(IBD, BLK, RANK),
        item_bucket.reshape(IBD, BLK),
        propensity.reshape(1, -1),
        tile_blocks,
        positives.T,
    )
    new_users, new_items = pl.pallas_call(
        hand_over,
        out_shape=(
            jax.ShapeDtypeStruct(user_factors.shape, BF16),
            jax.ShapeDtypeStruct((IBD, BLK, RANK), BF16),
        ),
        in_specs=[vmem, vmem],
        out_specs=(vmem, vmem),
    )(new_users, new_items)
    return new_users, new_items.reshape(item_factors.shape)


def solution(mesh):
    na = mesh.shape["user"] // NX // 2
    return jax.shard_map(
        functools.partial(body, na),
        mesh=mesh,
        in_specs=(
            P("user", None),
            P(("user", "item"), None),
            P(("user", "item")),
            P(),
            P("user", "item"),
            P("user", "item"),
        ),
        out_specs=(P("user", None), P(("user", "item"), None)),
        check_vma=False,
    )
```

```python
import functools

import jax
import jax.numpy as jnp
from jax import lax
from jax.experimental import pallas as pl
from jax.experimental.pallas import tpu as pltpu
from jax.sharding import PartitionSpec as P

BLK = 128
STEP_USER = 0.02
STEP_ITEM = 0.1
DECAY = 0.1
MESH = pl.DeviceIdType.MESH
F32 = jnp.float32
BF16 = jnp.bfloat16

NX = 4
NY = 4
IBD = 6
RANK = 256
HB = IBD // 2
HALF = HB * BLK
QR = BLK // NY
NO = 2 * NX
ZB = 2
ZROWS = 3 * BLK // 2
CUT = BLK // 2
LAG1 = 4
LAG2 = 5


def nt(a, b):
    return lax.dot_general(a, b, (((1,), (1,)), ((), ())), preferred_element_type=F32)


def nn(a, b):
    return lax.dot_general(a, b, (((1,), (0,)), ((), ())), preferred_element_type=F32)


def kernel(na, u_ref, it_ref, bk_in, prop_in, tb_in, pos_in, ou_ref, oi_ref,
           bk_ref, prop_ref, tb_ref, pos_ref,
           cm, cr, idv, ids, items, invp, invrow, invcol, ua, ub, gs, yr, zs_buf, zr, slot, prv, lst,
           cs, ccr, xs, zrec, xrec, xrec1, psum, prec, own_sum, fin,
           c_s, c_r, sm_sem, ix_s, ix_r, iz_s, iz_r, jx_s, jx_r, jz_s, jz_r, f_s, f_r, e_s, e_r,
           p_s, p_r, pz_s, pz_r, pf_s, pf_r,
           az_s, az_r, ay_s, ay_r, ry_s, ry_r, rz_s, rz_r, bz_s, bz_r, by_s, by_r,
           g_s, g_r, x_s, x_r, xb_s, xb_r, w_s, w_r, v_s, v_r, t_s, t_r, o_s, o_r, l_sem):
    user = lax.axis_index("user")
    y = lax.axis_index("item")
    r = lax.axis_index("rep")
    z = user // NX
    x = user % NX
    m = z // 2
    p = z % 2
    own = NX * p
    far = NX - own
    k0 = own + x
    c = RANK ** -0.5

    def zdev(mm):
        return ((2 * mm + p) * NX + x, y, r)

    def xdev(xx):
        return (z * NX + xx, y, r)

    def ydev(yy):
        return (user, yy, r)

    sib = (user, y, 1 - r)
    mate = ((2 * m + 1 - p) * NX + x, y, r)

    def rc(src, dst, ss, rs, dev):
        return pltpu.make_async_remote_copy(
            src_ref=src, dst_ref=dst, send_sem=ss, recv_sem=rs, device_id=dev, device_id_type=MESH)

    def step(i):
        return na // 2 + (2 * (i % 2) - 1) * ((i + 1) // 2)

    def peer(i):
        return lax.rem(m + step(i), na)

    def source(i):
        return lax.rem(m + 2 * na - step(i), na)

    def off(base, i, n):
        return lax.rem(base + i, n)

    barrier = pltpu.get_barrier_semaphore()

    def greet(i, carry):
        pl.semaphore_signal(barrier, inc=1, device_id=zdev(peer(i)), device_id_type=MESH)
        return carry

    lax.fori_loop(0, na - 1, greet, 0)
    for d in range(1, NX):
        pl.semaphore_signal(barrier, inc=1, device_id=xdev(off(x, d, NX)), device_id_type=MESH)
    for d in range(1, NY):
        pl.semaphore_signal(barrier, inc=1, device_id=ydev(off(y, d, NY)), device_id_type=MESH)
    pl.semaphore_signal(barrier, inc=1, device_id=sib, device_id_type=MESH)
    pl.semaphore_signal(barrier, inc=1, device_id=mate, device_id_type=MESH)

    b0 = pl.multiple_of(r * BLK, BLK)
    q0 = pl.multiple_of(y * QR, QR)
    h0 = r * HB
    own_items = pltpu.make_async_copy(it_ref, items.at[k0], l_sem.at[0])
    own_items.start()
    own_users = pltpu.make_async_copy(u_ref.at[pl.ds(b0, BLK)], ua.at[m], l_sem.at[1])
    own_users.start()

    small = [pltpu.make_async_copy(a, b, l_sem.at[2 + n]) for n, (a, b) in enumerate(
        ((tb_in, tb_ref), (pos_in, pos_ref), (bk_in, bk_ref), (prop_in, prop_ref)))]
    for copy in small:
        copy.start()
    for copy in small:
        copy.wait()

    tb = tb_ref[pl.ds(r, 1), :]
    owner = (tb * 2731) >> 16
    local = tb - owner * (NY * IBD) - y * IBD
    ow_rows = lax.broadcasted_iota(jnp.int32, (na * NO, tb.shape[1]), 0)
    hot = jnp.where(ow_rows == owner, local + 1, 0)
    packed = 256 * jnp.broadcast_to(jnp.max(hot, axis=1, keepdims=True), (na * NO, BLK))
    for t in range(tb.shape[1]):
        found = jnp.maximum(pos_ref[t:t + 1, pl.ds(b0, BLK)], -1) + 1
        packed = packed + jnp.where(hot[:, t:t + 1] > 0, found, 0)
    for mm in range(na):
        cm[mm] = packed[mm * NO:(mm + 1) * NO, :]

    bk = bk_ref[...]
    inv = jnp.zeros((IBD, BLK), F32)
    for b in range(16):
        inv = inv + jnp.where(bk == b, 1.0 / jnp.full((IBD, BLK), prop_ref[0, b], F32), 0.0)
    invp[k0, 0:IBD, :] = inv * (2.0 * c)
    cr[m] = cm[m]

    def code_copy(i):
        mm = peer(i)
        return rc(cm.at[mm], cr.at[m], c_s.at[mm], c_r.at[m], zdev(mm))

    def az_copy(i):
        mm = peer(i)
        part = ua.at[m, pl.ds(q0, QR)]
        return rc(part, part, az_s.at[mm], az_r.at[m], zdev(mm))

    def ix_copy(xx):
        part = items.at[k0, pl.ds(h0, HB)]
        return rc(part, part, ix_s.at[xx], ix_r.at[x], xdev(xx))

    def ix_in(xx):
        part = items.at[own + xx, pl.ds(h0, HB)]
        return rc(part, part, ix_s.at[xx], ix_r.at[xx], xdev(xx))

    def iz_copy(k):
        part = items.at[k, pl.ds(h0, HB)]
        return rc(part, part, iz_s, iz_r, mate)

    def jz_copy(k, xx):
        part = items.at[k, pl.ds(h0 + ZB, HB - ZB)]
        return rc(part, part, jz_s.at[xx], jz_r.at[xx], mate)

    def jx_copy(xx):
        part = items.at[far + x, pl.ds(h0, ZB)]
        return rc(part, part, jx_s.at[xx], jx_r.at[x], xdev(xx))

    def jx_in(xx):
        part = items.at[far + xx, pl.ds(h0, ZB)]
        return rc(part, part, jx_s.at[xx], jx_r.at[xx], xdev(xx))

    def core_items(k, start):
        part = items.at[k, pl.ds(start, HB)]
        return rc(part, part, f_s.at[k], f_r.at[k], sib)

    def core_part(k, start, count, ss, rs):
        part = items.at[k, pl.ds(start, count)]
        return rc(part, part, ss, rs, sib)

    def core_far(xx, start, last):
        if last:
            return core_part(far + xx, start + ZB, HB - ZB, e_s.at[xx], e_r.at[xx])
        return core_part(far + xx, start, ZB, f_s.at[far + xx], f_r.at[far + xx])

    def p_copy(k, xx, ss, rs, slot):
        return rc(invp.at[k], invp.at[k], ss.at[xx], rs.at[slot], xdev(xx))

    def pz_copy(k):
        return rc(invp.at[k], invp.at[k], pz_s, pz_r, mate)

    own_users.wait()
    own_items.wait()
    pl.semaphore_wait(barrier, na - 1 + NX - 1 + NY - 1 + 2)

    def send_users(i, carry):
        az_copy(i).start()
        return carry

    def send_codes(i, carry):
        code_copy(i).start()
        return carry

    iz_copy(k0).start()
    for d in (1, 3, 2):
        ix_copy(off(x, d, NX)).start()
    lax.fori_loop(0, na - 1, send_users, 0)
    lax.fori_loop(0, na - 1, send_codes, 0)
    for d in (2, 1, 3):
        xx = off(x, d, NX)
        p_copy(k0, xx, p_s, p_r, x).start()
    pz_copy(k0).start()

    def forward_y(buf, mm, ss, rs):
        part = buf.at[mm, pl.ds(q0, QR)]
        for d in (2, 1, 3):
            rc(part, part, ss.at[mm], rs.at[mm], ydev(off(y, d, NY))).start()

    def three(buf, mm, ss, rs):
        part = buf.at[mm, pl.ds(0, QR * (NY - 1))]
        return rc(part, part, ss.at[mm], rs.at[mm], ydev(off(y, 1, NY)))

    def arrive_z(buf, mm, ss, rs):
        part = buf.at[mm, pl.ds(q0, QR)]
        rc(part, part, ss.at[mm], rs.at[mm], zdev(mm)).wait_recv()

    def forward_first(i, carry):
        mm = source(na - 2 - i)
        arrive_z(ua, mm, az_s, az_r)
        forward_y(ua, mm, ay_s, ay_r)
        return carry

    def forward_own(xx):
        ix_in(xx).wait_recv()
        jz_copy(own + xx, xx).start()
        core_items(own + xx, h0).start()

    iz_copy(far + x).wait_recv()
    for d in (2, 1, 3):
        jx_copy(off(x, d, NX)).start()
    core_items(far + x, h0).start()
    lax.fori_loop(0, 2, forward_first, 0)
    forward_own(off(x, 1, NX))
    forward_own(off(x, 3, NX))
    lax.fori_loop(2, 4, forward_first, 0)
    forward_own(off(x, 2, NX))
    pz_copy(far + x).wait_recv()
    for d in (2, 1, 3):
        xx = off(x, d, NX)
        p_copy(far + x, xx, pf_s, pf_r, x).start()
    lax.fori_loop(4, na - 1, forward_first, 0)
    for d in (1, 3, 2):
        xx = off(x, d, NX)
        p_copy(own + xx, xx, p_s, p_r, xx).wait_recv()
        p_copy(far + xx, xx, pf_s, pf_r, xx).wait_recv()

    def take_codes(i, carry):
        mm = source(i)
        rc(cm.at[mm], cr.at[mm], c_s.at[mm], c_r.at[mm], zdev(mm)).wait_recv()
        return carry

    lax.fori_loop(0, na - 1, take_codes, 0)
    idv[...] = jnp.zeros_like(idv)
    for mm in range(na):
        idv[mm:mm + 1, 0:NO] = jnp.transpose(cr[mm])[0:1, :]
    to_smem = pltpu.make_async_copy(idv, ids, sm_sem)
    to_smem.start()
    for k in range(NO):
        for j in range(IBD):
            invrow[k, j] = jnp.broadcast_to(invp[k, j:j + 1, :], (8, BLK))
    to_smem.wait()

    for d in (1, 3, 2):
        xx = off(x, d, NX)
        jz_copy(far + xx, xx).wait_recv()
        core_far(xx, h0, True).start()
    for d in (1, 3, 2):
        xx = off(x, d, NX)
        jx_in(xx).wait_recv()
        core_far(xx, h0, False).start()
    o0 = (1 - r) * HB
    core_items(far + x, o0).wait_recv()
    for d in (1, 3, 2):
        xx = off(x, d, NX)
        core_items(own + xx, o0).wait_recv()
        core_far(xx, o0, True).wait_recv()
        core_far(xx, o0, False).wait_recv()

    lane_f = lax.broadcasted_iota(jnp.int32, (BLK, BLK), 1).astype(F32)
    sub = lax.broadcasted_iota(jnp.int32, (BLK, BLK), 0)

    def pick(mm, k):
        code = ids[mm, k] >> 8
        j = jnp.maximum(code - 1, 0)
        flat = jnp.where(code > 0, 2.0 * c, 0.0).astype(F32)
        return code, j, items[k, j], flat

    def grads(mm):
        users = ua[mm]
        cols = jnp.transpose(((cr[mm] & 255) - 1).astype(F32))
        total = jnp.zeros((BLK, RANK), F32)
        for part in range(NO // NX):
            picks = [pick(mm, part * NX + q) for q in range(NX)]
            stack = jnp.concatenate([t[2] for t in picks], axis=0)
            scores = nt(users, stack)
            hs = []
            for q in range(NX):
                k = part * NX + q
                code, j, block, flat = picks[q]
                s = scores[:, q * BLK:(q + 1) * BLK]
                hit = cols[:, k:k + 1] == lane_f
                w = invrow[k, j][0:1, :]
                margin = jnp.maximum(1.0 + s * jnp.where(hit, -c, c), 0.0)
                hs.append((margin * jnp.where(hit, -w, flat)).astype(BF16))
            total = total + nn(jnp.concatenate(hs, axis=1), stack)
        return total

    def ry_copy(mm, d):
        yy = off(y, d, NY)
        return rc(gs.at[mm, pl.ds(pl.multiple_of(yy * QR, QR), QR)], yr.at[mm, pl.ds(q0, QR)],
                  ry_s.at[mm], ry_r.at[mm], ydev(yy))

    def rz_copy(mm):
        return rc(zs_buf.at[mm], zr.at[m], rz_s.at[mm], rz_r.at[m], zdev(mm))

    def sum_y(mm):
        part = yr.at[mm, pl.ds(0, QR * (NY - 1))]
        rc(part, part, ry_s.at[mm], ry_r.at[mm], ydev(off(y, 1, NY))).wait_recv()
        total = gs[mm, pl.ds(q0, QR), :].astype(F32)
        for d in range(1, NY):
            total = total + yr[mm, pl.ds(pl.multiple_of(off(y, d, NY) * QR, QR), QR), :].astype(F32)
        return total

    def first_pass(i, carry):
        @pl.when(i < na)
        def _():
            mm = peer(i)

            @pl.when(i < na - 1)
            def _():
                three(ua, mm, ay_s, ay_r).wait_recv()

            gs[mm] = grads(mm).astype(BF16)
            for d in (2, 1, 3):
                ry_copy(mm, d).start()

        @pl.when(i >= LAG1)
        def _():
            mm = peer(i - LAG1)
            total = sum_y(mm)

            @pl.when(i < na - 1 + LAG1)
            def _():
                zs_buf[mm] = total.astype(BF16)
                rz_copy(mm).start()

            @pl.when(i == na - 1 + LAG1)
            def _():
                own_sum[...] = total

        return carry

    lax.fori_loop(0, na + LAG1, first_pass, 0)

    def chain(k, carry):
        codes = [ids[source(na - 1 - i), k] >> 8 for i in range(na)]
        for i in range(na):
            before = 0
            for e in range(i):
                before = jnp.where(codes[e] == codes[i], e + 1, before)
            prv[k, i] = jnp.int32(before)
        for j in range(IBD):
            last = 0
            for i in range(na):
                last = jnp.where(codes[i] == j + 1, i + 1, last)
            lst[k, j] = last
        cols = jnp.transpose(invp[k])
        for j in range(IBD):
            invcol[k, j] = jnp.broadcast_to(cols[:, j:j + 1], (BLK, BLK))
        slot[k, 0] = jnp.zeros((BLK, RANK), F32)
        return carry

    lax.fori_loop(0, NO, chain, 0)

    def gather_sum(i, carry):
        mm = source(i)
        rc(zs_buf.at[mm], zr.at[mm], rz_s.at[mm], rz_r.at[mm], zdev(mm)).wait_recv()
        own_sum[...] += zr[mm].astype(F32)
        return carry

    lax.fori_loop(0, na - 1, gather_sum, 0)

    old = ua[m, pl.ds(q0, QR), :].astype(F32)
    ub[m, pl.ds(q0, QR), :] = (old - STEP_USER * (own_sum[...] + DECAY * old)).astype(BF16)

    def bz_copy(i):
        mm = peer(i)
        part = ub.at[m, pl.ds(q0, QR)]
        return rc(part, part, bz_s.at[mm], bz_r.at[m], zdev(mm))

    def send_new(i, carry):
        bz_copy(na - 2 - i).start()
        return carry

    lax.fori_loop(0, na - 1, send_new, 0)
    forward_y(ub, m, by_s, by_r)

    def expand(i, mm):
        users = ub[mm]
        for part in range(NO // NX):
            picks = [pick(mm, part * NX + q) for q in range(NX)]
            scores = nt(jnp.concatenate([t[2] for t in picks], axis=0), users)
            hs = []
            for q in range(NX):
                k = part * NX + q
                code, j, block, flat = picks[q]
                s = scores[q * BLK:(q + 1) * BLK]
                hit = (cr[mm, k:k + 1, :] & 255) - 1 == sub
                margin = jnp.maximum(1.0 + s * jnp.where(hit, -c, c), 0.0)
                hs.append((margin * jnp.where(hit, -invcol[k, j], flat)).astype(BF16))
            terms = nn(jnp.concatenate(hs, axis=0), users)
            for q in range(NX):
                k = part * NX + q
                slot[k, i + 1] = terms[q * BLK:(q + 1) * BLK] + slot[k, prv[k, i]]

    def second_pass(i, carry):
        @pl.when(jnp.logical_and(i > 0, i < na))
        def _():
            mm = source(na - 1 - i)
            arrive_z(ub, mm, bz_s, bz_r)
            forward_y(ub, mm, by_s, by_r)

        @pl.when(i >= LAG2)
        def _():
            mm = source(na - 1 - (i - LAG2))
            three(ub, mm, by_s, by_r).wait_recv()
            expand(i - LAG2, mm)

        return carry

    lax.fori_loop(0, na + LAG2, second_pass, 0)

    keep_u = pltpu.make_async_copy(ub.at[m], ou_ref.at[pl.ds(b0, BLK)], l_sem.at[0])
    keep_u.start()
    out_u = rc(ub.at[m], ou_ref.at[pl.ds(b0, BLK)], o_s.at[0], o_r.at[0], sib)
    out_u.start()

    def item_sum(k, b):
        return slot[k, lst[k, b]]

    def core_copy(k):
        return rc(cs.at[k], ccr.at[k], g_s.at[k], g_r.at[k], sib)

    def other_half(k):
        for b in range(HB):
            cs[k, b * BLK:(b + 1) * BLK, :] = item_sum(k, o0 + b).astype(BF16)
        core_copy(k).start()

    def both(k):
        core_copy(k).wait_recv()
        for b in range(HB):
            rows = slice(b * BLK, (b + 1) * BLK)
            xs[k, rows, :] = (item_sum(k, h0 + b) + ccr[k, rows, :].astype(F32)).astype(BF16)

    def w_copy(xx):
        return rc(xs.at[far + xx, pl.ds(0, ZROWS)], zrec.at[xx], w_s.at[xx], w_r.at[xx], mate)

    def w_in(xx):
        return rc(xs.at[own + xx, pl.ds(0, ZROWS)], zrec.at[xx], w_s.at[xx], w_r.at[xx], mate)

    def v_copy(xx):
        return rc(xs.at[far + xx, pl.ds(ZROWS, HALF - ZROWS)], xrec1.at[x], v_s.at[xx], v_r.at[x], xdev(xx))

    def xa_copy(xx):
        rows = pl.ds(ZROWS, HALF - ZROWS)
        return rc(xs.at[own + xx, rows], xrec.at[x, rows], x_s.at[xx], x_r.at[x], xdev(xx))

    def xb_copy(xx):
        rows = pl.ds(0, ZROWS)
        return rc(xs.at[own + xx, rows], xrec.at[x, rows], xb_s.at[xx], xb_r.at[x], xdev(xx))

    order = [off(x, d, NX) for d in (2, 1, 3, 0)]
    owners = [far + xx for xx in order] + [own + xx for xx in order]
    other_half(owners[0])
    other_half(owners[1])
    for n, k in enumerate(owners):
        if n + 2 < NO:
            other_half(owners[n + 2])
        both(k)
        xx = order[n % NX]
        if n < NX:
            w_copy(xx).start()
            if n < NX - 1:
                v_copy(xx).start()
        elif n < NO - 1:
            xa_copy(xx).start()

    for n, xx in enumerate(order):
        k = own + xx
        w_in(xx).wait_recv()
        rows = pl.ds(0, ZROWS)
        xs[k, rows, :] = (xs[k, rows, :].astype(F32) + zrec[xx].astype(F32)).astype(BF16)
        if n < NX - 1:
            xb_copy(xx).start()

    part = xs[far + x, pl.ds(ZROWS, HALF - ZROWS), :].astype(F32)
    for d in (1, 3, 2):
        xx = off(x, d, NX)
        rc(xrec1.at[xx], xrec1.at[xx], v_s.at[xx], v_r.at[xx], xdev(xx)).wait_recv()
        part = part + xrec1[xx].astype(F32)
    psum[...] = part.astype(BF16)
    to_mate = rc(psum, prec, t_s, t_r, mate)
    to_mate.start()

    for d in (1, 3, 2):
        xx = off(x, d, NX)
        lower, upper = xrec.at[xx, pl.ds(0, ZROWS)], xrec.at[xx, pl.ds(ZROWS, HALF - ZROWS)]
        rc(upper, upper, x_s.at[xx], x_r.at[xx], xdev(xx)).wait_recv()
        rc(lower, lower, xb_s.at[xx], xb_r.at[xx], xdev(xx)).wait_recv()
    to_mate.wait_recv()
    def out_item(b, start):
        return rc(fin.at[b], oi_ref.at[start + b], o_s.at[1 + b], o_r.at[1 + b], sib)

    def keep_item(b):
        return pltpu.make_async_copy(fin.at[b], oi_ref.at[h0 + b], l_sem.at[1 + b])

    for b in range(2 * HB):
        rows = pl.ds(b * CUT, CUT)
        total = xs[k0, rows, :].astype(F32)
        for d in range(1, NX):
            total = total + xrec[off(x, d, NX), rows, :].astype(F32)
        if b * CUT >= ZROWS:
            total = total + prec[pl.ds(b * CUT - ZROWS, CUT), :].astype(F32)
        piece = pl.ds(b % 2 * CUT, CUT)
        olds = items[k0, h0 + b // 2, piece, :].astype(F32)
        fin[b // 2, piece, :] = (olds - STEP_ITEM * (total + DECAY * olds)).astype(BF16)
        if b % 2:
            out_item(b // 2, h0).start()
            keep_item(b // 2).start()

    iz_copy(k0).wait_send()
    pz_copy(k0).wait_send()
    to_mate.wait_send()
    core_items(far + x, h0).wait_send()
    for d in range(NX):
        xx = off(x, d, NX)
        core_copy(own + xx).wait_send()
        core_copy(far + xx).wait_send()
        w_copy(xx).wait_send()
        if d:
            ix_copy(xx).wait_send()
            jx_copy(xx).wait_send()
            jz_copy(own + xx, xx).wait_send()
            core_items(own + xx, h0).wait_send()
            core_far(xx, h0, True).wait_send()
            core_far(xx, h0, False).wait_send()
            p_copy(k0, xx, p_s, p_r, x).wait_send()
            p_copy(far + x, xx, pf_s, pf_r, x).wait_send()
            v_copy(xx).wait_send()
            xa_copy(xx).wait_send()
            xb_copy(xx).wait_send()

    def sent(i, carry):
        code_copy(i).wait_send()
        az_copy(i).wait_send()
        bz_copy(i).wait_send()
        mm = peer(i)
        three(ua, mm, ay_s, ay_r).wait_send()
        rz_copy(mm).wait_send()
        return carry

    lax.fori_loop(0, na - 1, sent, 0)

    def sent_all(i, carry):
        three(ub, i, by_s, by_r).wait_send()
        three(gs, i, ry_s, ry_r).wait_send()
        return carry

    lax.fori_loop(0, na, sent_all, 0)
    out_u.wait_send()
    keep_u.wait()
    other_b = pl.multiple_of((1 - r) * BLK, BLK)
    rc(ub.at[m], ou_ref.at[pl.ds(other_b, BLK)], o_s.at[0], o_r.at[0], sib).wait_recv()
    for b in range(HB):
        keep_item(b).wait()
        out_item(b, h0).wait_send()
        out_item(b, o0).wait_recv()


def hand_over(u_ref, i_ref, ou_ref, oi_ref):
    ou_ref[...] = u_ref[...]
    oi_ref[...] = i_ref[...]


def body(na, user_factors, item_factors, item_bucket, propensity, tile_blocks, positives):
    dma = pltpu.SemaphoreType.DMA
    V = pltpu.VMEM
    scratch = [
        V((IBD, BLK), jnp.int32),
        pltpu.SMEM((1, propensity.shape[0]), F32),
        V(tile_blocks.shape, jnp.int32),
        V((positives.shape[1], positives.shape[0]), jnp.int32),
        V((na, NO, BLK), jnp.int32),
        V((na, NO, BLK), jnp.int32),
        V((na, BLK), jnp.int32),
        pltpu.SMEM((na, BLK), jnp.int32),
        V((NO, IBD, BLK, RANK), BF16),
        V((NO, 8, BLK), F32),
        V((NO, IBD, 8, BLK), F32),
        V((NO, IBD, BLK, BLK), F32),
        V((na, BLK, RANK), BF16),
        V((na, BLK, RANK), BF16),
        V((na, BLK, RANK), BF16),
        V((na, BLK, RANK), BF16),
        V((na, QR, RANK), BF16),
        V((na, QR, RANK), BF16),
        V((NO, na + 1, BLK, RANK), F32),
        pltpu.SMEM((NO, na), jnp.int32),
        pltpu.SMEM((NO, IBD), jnp.int32),
        V((NO, HALF, RANK), BF16),
        V((NO, HALF, RANK), BF16),
        V((NO, HALF, RANK), BF16),
        V((NX, ZROWS, RANK), BF16),
        V((NX, HALF, RANK), BF16),
        V((NX, HALF - ZROWS, RANK), BF16),
        V((HALF - ZROWS, RANK), BF16),
        V((HALF - ZROWS, RANK), BF16),
        V((QR, RANK), F32),
        V((HB, BLK, RANK), BF16),
        dma((na,)), dma((na,)), dma,
        dma((NX,)), dma((NX,)), dma, dma, dma((NX,)), dma((NX,)), dma((NX,)), dma((NX,)), dma((NO,)), dma((NO,)),
        dma((NX,)), dma((NX,)),
        dma((NX,)), dma((NX,)), dma, dma, dma((NX,)), dma((NX,)),
        dma((na,)), dma((na,)), dma((na,)), dma((na,)),
        dma((na,)), dma((na,)), dma((na,)), dma((na,)),
        dma((na,)), dma((na,)), dma((na,)), dma((na,)),
        dma((NO,)), dma((NO,)), dma((NX,)), dma((NX,)), dma((NX,)), dma((NX,)),
        dma((NX,)), dma((NX,)), dma((NX,)), dma((NX,)), dma, dma,
        dma((1 + HB,)), dma((1 + HB,)), dma((6,)),
    ]
    vmem = pl.BlockSpec(memory_space=pltpu.VMEM)
    anywhere = pl.BlockSpec(memory_space=pl.ANY)
    new_users, new_items = pl.pallas_call(
        functools.partial(kernel, na),
        out_shape=(
            jax.ShapeDtypeStruct(user_factors.shape, BF16),
            jax.ShapeDtypeStruct((IBD, BLK, RANK), BF16),
        ),
        in_specs=[anywhere] * 6,
        out_specs=(anywhere, anywhere),
        scratch_shapes=scratch,
        compiler_params=pltpu.CompilerParams(
            collective_id=0, has_side_effects=True, vmem_limit_bytes=56 << 20),
    )(
        user_factors,
        item_factors.reshape(IBD, BLK, RANK),
        item_bucket.reshape(IBD, BLK),
        propensity.reshape(1, -1),
        tile_blocks,
        positives.T,
    )
    new_users, new_items = pl.pallas_call(
        hand_over,
        out_shape=(
            jax.ShapeDtypeStruct(user_factors.shape, BF16),
            jax.ShapeDtypeStruct((IBD, BLK, RANK), BF16),
        ),
        in_specs=[vmem, vmem],
        out_specs=(vmem, vmem),
    )(new_users, new_items)
    return new_users, new_items.reshape(item_factors.shape)


def solution(mesh):
    na = mesh.shape["user"] // NX // 2
    return jax.shard_map(
        functools.partial(body, na),
        mesh=mesh,
        in_specs=(
            P("user", None),
            P(("user", "item"), None),
            P(("user", "item")),
            P(),
            P("user", "item"),
            P("user", "item"),
        ),
        out_specs=(P("user", None), P(("user", "item"), None)),
        check_vma=False,
    )
```

```python
import functools

import jax
import jax.numpy as jnp
from jax import lax
from jax.experimental import pallas as pl
from jax.experimental.pallas import tpu as pltpu
from jax.sharding import PartitionSpec as P

BLK = 128
STEP_USER = 0.02
STEP_ITEM = 0.1
DECAY = 0.1
MESH = pl.DeviceIdType.MESH
F32 = jnp.float32
BF16 = jnp.bfloat16

NX = 4
NY = 4
IBD = 6
RANK = 256
HB = IBD // 2
HALF = HB * BLK
QR = BLK // NY
NO = 2 * NX
ZB = 2
ZROWS = 3 * BLK // 2
CUT = BLK // 2
LAG1 = 4
LAG2 = 5


def nt(a, b):
    return lax.dot_general(a, b, (((1,), (1,)), ((), ())), preferred_element_type=F32)


def nn(a, b):
    return lax.dot_general(a, b, (((1,), (0,)), ((), ())), preferred_element_type=F32)


def kernel(na, u_ref, it_ref, bk_in, prop_in, tb_in, pos_in, ou_ref, oi_ref,
           bk_ref, prop_ref, tb_ref, pos_ref,
           cm, cr, idv, ids, items, invp, invrow, invcol, ua, ub, gs, yr, zs_buf, zr, slot, prv, lst,
           cs, ccr, xs, zrec, xrec, xrec1, psum, prec, own_sum, fin,
           c_s, c_r, sm_sem, ix_s, ix_r, iz_s, iz_r, jx_s, jx_r, jz_s, jz_r, f_s, f_r, e_s, e_r,
           p_s, p_r, pz_s, pz_r, pf_s, pf_r,
           az_s, az_r, ay_s, ay_r, ry_s, ry_r, rz_s, rz_r, bz_s, bz_r, by_s, by_r,
           g_s, g_r, x_s, x_r, xb_s, xb_r, w_s, w_r, v_s, v_r, t_s, t_r, o_s, o_r, l_sem):
    user = lax.axis_index("user")
    y = lax.axis_index("item")
    r = lax.axis_index("rep")
    z = user // NX
    x = user % NX
    m = z // 2
    p = z % 2
    own = NX * p
    far = NX - own
    k0 = own + x
    c = RANK ** -0.5

    def zdev(mm):
        return ((2 * mm + p) * NX + x, y, r)

    def xdev(xx):
        return (z * NX + xx, y, r)

    def ydev(yy):
        return (user, yy, r)

    sib = (user, y, 1 - r)
    mate = ((2 * m + 1 - p) * NX + x, y, r)

    def rc(src, dst, ss, rs, dev):
        return pltpu.make_async_remote_copy(
            src_ref=src, dst_ref=dst, send_sem=ss, recv_sem=rs, device_id=dev, device_id_type=MESH)

    def step(i):
        return na // 2 + (2 * (i % 2) - 1) * ((i + 1) // 2)

    def peer(i):
        return lax.rem(m + step(i), na)

    def source(i):
        return lax.rem(m + 2 * na - step(i), na)

    def off(base, i, n):
        return lax.rem(base + i, n)

    b0 = pl.multiple_of(r * BLK, BLK)
    q0 = pl.multiple_of(y * QR, QR)
    h0 = r * HB
    own_items = pltpu.make_async_copy(it_ref, items.at[k0], l_sem.at[0])
    own_items.start()
    own_users = pltpu.make_async_copy(u_ref.at[pl.ds(b0, BLK)], ua.at[m], l_sem.at[1])
    own_users.start()

    small = [pltpu.make_async_copy(a, b, l_sem.at[2 + n]) for n, (a, b) in enumerate(
        ((tb_in, tb_ref), (pos_in, pos_ref), (bk_in, bk_ref), (prop_in, prop_ref)))]
    for copy in small:
        copy.start()

    barrier = pltpu.get_barrier_semaphore()

    def greet(i, carry):
        pl.semaphore_signal(barrier, inc=1, device_id=zdev(peer(i)), device_id_type=MESH)
        return carry

    lax.fori_loop(0, na - 1, greet, 0)
    for d in range(1, NX):
        pl.semaphore_signal(barrier, inc=1, device_id=xdev(off(x, d, NX)), device_id_type=MESH)
    for d in range(1, NY):
        pl.semaphore_signal(barrier, inc=1, device_id=ydev(off(y, d, NY)), device_id_type=MESH)
    pl.semaphore_signal(barrier, inc=1, device_id=sib, device_id_type=MESH)
    pl.semaphore_signal(barrier, inc=1, device_id=mate, device_id_type=MESH)

    for copy in small:
        copy.wait()

    tb = tb_ref[pl.ds(r, 1), :]
    owner = (tb * 2731) >> 16
    local = tb - owner * (NY * IBD) - y * IBD
    ow_rows = lax.broadcasted_iota(jnp.int32, (na * NO, tb.shape[1]), 0)
    hot = jnp.where(ow_rows == owner, local + 1, 0)
    packed = 256 * jnp.broadcast_to(jnp.max(hot, axis=1, keepdims=True), (na * NO, BLK))
    for t in range(tb.shape[1]):
        found = jnp.maximum(pos_ref[t:t + 1, pl.ds(b0, BLK)], -1) + 1
        packed = packed + jnp.where(hot[:, t:t + 1] > 0, found, 0)
    for mm in range(na):
        cm[mm] = packed[mm * NO:(mm + 1) * NO, :]

    bk = bk_ref[...]
    inv = jnp.zeros((IBD, BLK), F32)
    for b in range(16):
        inv = inv + jnp.where(bk == b, 1.0 / jnp.full((IBD, BLK), prop_ref[0, b], F32), 0.0)
    invp[k0, 0:IBD, :] = inv * (2.0 * c)
    cr[m] = cm[m]

    def code_copy(i):
        mm = peer(i)
        return rc(cm.at[mm], cr.at[m], c_s.at[mm], c_r.at[m], zdev(mm))

    def az_copy(i):
        mm = peer(i)
        part = ua.at[m, pl.ds(q0, QR)]
        return rc(part, part, az_s.at[mm], az_r.at[m], zdev(mm))

    def ix_copy(xx):
        part = items.at[k0, pl.ds(h0, HB)]
        return rc(part, part, ix_s.at[xx], ix_r.at[x], xdev(xx))

    def ix_in(xx):
        part = items.at[own + xx, pl.ds(h0, HB)]
        return rc(part, part, ix_s.at[xx], ix_r.at[xx], xdev(xx))

    def iz_copy(k):
        part = items.at[k, pl.ds(h0, HB)]
        return rc(part, part, iz_s, iz_r, mate)

    def jz_copy(k, xx):
        part = items.at[k, pl.ds(h0 + ZB, HB - ZB)]
        return rc(part, part, jz_s.at[xx], jz_r.at[xx], mate)

    def jx_copy(xx):
        part = items.at[far + x, pl.ds(h0, ZB)]
        return rc(part, part, jx_s.at[xx], jx_r.at[x], xdev(xx))

    def jx_in(xx):
        part = items.at[far + xx, pl.ds(h0, ZB)]
        return rc(part, part, jx_s.at[xx], jx_r.at[xx], xdev(xx))

    def core_items(k, start):
        part = items.at[k, pl.ds(start, HB)]
        return rc(part, part, f_s.at[k], f_r.at[k], sib)

    def core_part(k, start, count, ss, rs):
        part = items.at[k, pl.ds(start, count)]
        return rc(part, part, ss, rs, sib)

    def core_far(xx, start, last):
        if last:
            return core_part(far + xx, start + ZB, HB - ZB, e_s.at[xx], e_r.at[xx])
        return core_part(far + xx, start, ZB, f_s.at[far + xx], f_r.at[far + xx])

    def p_copy(k, xx, ss, rs, slot):
        return rc(invp.at[k], invp.at[k], ss.at[xx], rs.at[slot], xdev(xx))

    def pz_copy(k):
        return rc(invp.at[k], invp.at[k], pz_s, pz_r, mate)

    own_users.wait()
    own_items.wait()
    pl.semaphore_wait(barrier, na - 1 + NX - 1 + NY - 1 + 2)

    def send_users(i, carry):
        az_copy(i).start()
        return carry

    def send_codes(i, carry):
        code_copy(i).start()
        return carry

    iz_copy(k0).start()
    for d in (1, 3, 2):
        ix_copy(off(x, d, NX)).start()
    lax.fori_loop(0, na - 1, send_users, 0)
    lax.fori_loop(0, na - 1, send_codes, 0)
    for d in (2, 1, 3):
        xx = off(x, d, NX)
        p_copy(k0, xx, p_s, p_r, x).start()
    pz_copy(k0).start()

    def forward_y(buf, mm, ss, rs):
        part = buf.at[mm, pl.ds(q0, QR)]
        for d in (2, 1, 3):
            rc(part, part, ss.at[mm], rs.at[mm], ydev(off(y, d, NY))).start()

    def three(buf, mm, ss, rs):
        part = buf.at[mm, pl.ds(0, QR * (NY - 1))]
        return rc(part, part, ss.at[mm], rs.at[mm], ydev(off(y, 1, NY)))

    def arrive_z(buf, mm, ss, rs):
        part = buf.at[mm, pl.ds(q0, QR)]
        rc(part, part, ss.at[mm], rs.at[mm], zdev(mm)).wait_recv()

    def forward_first(i, carry):
        mm = source(na - 2 - i)
        arrive_z(ua, mm, az_s, az_r)
        forward_y(ua, mm, ay_s, ay_r)
        return carry

    def forward_own(xx):
        ix_in(xx).wait_recv()
        jz_copy(own + xx, xx).start()
        core_items(own + xx, h0).start()

    iz_copy(far + x).wait_recv()
    for d in (2, 1, 3):
        jx_copy(off(x, d, NX)).start()
    core_items(far + x, h0).start()
    lax.fori_loop(0, 2, forward_first, 0)
    forward_own(off(x, 1, NX))
    forward_own(off(x, 3, NX))
    lax.fori_loop(2, 4, forward_first, 0)
    forward_own(off(x, 2, NX))
    pz_copy(far + x).wait_recv()
    for d in (2, 1, 3):
        xx = off(x, d, NX)
        p_copy(far + x, xx, pf_s, pf_r, x).start()
    lax.fori_loop(4, na - 1, forward_first, 0)
    for d in (1, 3, 2):
        xx = off(x, d, NX)
        p_copy(own + xx, xx, p_s, p_r, xx).wait_recv()
        p_copy(far + xx, xx, pf_s, pf_r, xx).wait_recv()

    def take_codes(i, carry):
        mm = source(i)
        rc(cm.at[mm], cr.at[mm], c_s.at[mm], c_r.at[mm], zdev(mm)).wait_recv()
        return carry

    lax.fori_loop(0, na - 1, take_codes, 0)
    idv[...] = jnp.zeros_like(idv)
    for mm in range(na):
        idv[mm:mm + 1, 0:NO] = jnp.transpose(cr[mm])[0:1, :]
    to_smem = pltpu.make_async_copy(idv, ids, sm_sem)
    to_smem.start()
    for k in range(NO):
        for j in range(IBD):
            invrow[k, j] = jnp.broadcast_to(invp[k, j:j + 1, :], (8, BLK))
    to_smem.wait()

    for d in (1, 3, 2):
        xx = off(x, d, NX)
        jz_copy(far + xx, xx).wait_recv()
        core_far(xx, h0, True).start()
    for d in (1, 3, 2):
        xx = off(x, d, NX)
        jx_in(xx).wait_recv()
        core_far(xx, h0, False).start()
    o0 = (1 - r) * HB
    core_items(far + x, o0).wait_recv()
    for d in (1, 3, 2):
        xx = off(x, d, NX)
        core_items(own + xx, o0).wait_recv()
        core_far(xx, o0, True).wait_recv()
        core_far(xx, o0, False).wait_recv()

    lane_f = lax.broadcasted_iota(jnp.int32, (BLK, BLK), 1).astype(F32)
    sub = lax.broadcasted_iota(jnp.int32, (BLK, BLK), 0)

    def pick(mm, k):
        code = ids[mm, k] >> 8
        j = jnp.maximum(code - 1, 0)
        flat = jnp.where(code > 0, 2.0 * c, 0.0).astype(F32)
        return code, j, items[k, j], flat

    def grads(mm):
        users = ua[mm]
        cols = jnp.transpose(((cr[mm] & 255) - 1).astype(F32))
        total = jnp.zeros((BLK, RANK), F32)
        for part in range(NO // NX):
            picks = [pick(mm, part * NX + q) for q in range(NX)]
            stack = jnp.concatenate([t[2] for t in picks], axis=0)
            scores = nt(users, stack)
            hs = []
            for q in range(NX):
                k = part * NX + q
                code, j, block, flat = picks[q]
                s = scores[:, q * BLK:(q + 1) * BLK]
                hit = cols[:, k:k + 1] == lane_f
                w = invrow[k, j][0:1, :]
                margin = jnp.maximum(1.0 + s * jnp.where(hit, -c, c), 0.0)
                hs.append((margin * jnp.where(hit, -w, flat)).astype(BF16))
            total = total + nn(jnp.concatenate(hs, axis=1), stack)
        return total

    def ry_copy(mm, d):
        yy = off(y, d, NY)
        return rc(gs.at[mm, pl.ds(pl.multiple_of(yy * QR, QR), QR)], yr.at[mm, pl.ds(q0, QR)],
                  ry_s.at[mm], ry_r.at[mm], ydev(yy))

    def rz_copy(mm):
        return rc(zs_buf.at[mm], zr.at[m], rz_s.at[mm], rz_r.at[m], zdev(mm))

    def sum_y(mm):
        part = yr.at[mm, pl.ds(0, QR * (NY - 1))]
        rc(part, part, ry_s.at[mm], ry_r.at[mm], ydev(off(y, 1, NY))).wait_recv()
        total = gs[mm, pl.ds(q0, QR), :].astype(F32)
        for d in range(1, NY):
            total = total + yr[mm, pl.ds(pl.multiple_of(off(y, d, NY) * QR, QR), QR), :].astype(F32)
        return total

    def first_pass(i, carry):
        @pl.when(i < na)
        def _():
            mm = peer(i)

            @pl.when(i < na - 1)
            def _():
                three(ua, mm, ay_s, ay_r).wait_recv()

            gs[mm] = grads(mm).astype(BF16)
            for d in (2, 1, 3):
                ry_copy(mm, d).start()

        @pl.when(i >= LAG1)
        def _():
            mm = peer(i - LAG1)
            total = sum_y(mm)

            @pl.when(i < na - 1 + LAG1)
            def _():
                zs_buf[mm] = total.astype(BF16)
                rz_copy(mm).start()

            @pl.when(i == na - 1 + LAG1)
            def _():
                own_sum[...] = total

        return carry

    lax.fori_loop(0, na + LAG1, first_pass, 0)

    def chain(k, carry):
        codes = [ids[source(na - 1 - i), k] >> 8 for i in range(na)]
        for i in range(na):
            before = 0
            for e in range(i):
                before = jnp.where(codes[e] == codes[i], e + 1, before)
            prv[k, i] = jnp.int32(before)
        for j in range(IBD):
            last = 0
            for i in range(na):
                last = jnp.where(codes[i] == j + 1, i + 1, last)
            lst[k, j] = last
        cols = jnp.transpose(invp[k])
        for j in range(IBD):
            invcol[k, j] = jnp.broadcast_to(cols[:, j:j + 1], (BLK, BLK))
        slot[k, 0] = jnp.zeros((BLK, RANK), F32)
        return carry

    lax.fori_loop(0, NO, chain, 0)

    def gather_sum(i, carry):
        mm = source(i)
        rc(zs_buf.at[mm], zr.at[mm], rz_s.at[mm], rz_r.at[mm], zdev(mm)).wait_recv()
        own_sum[...] += zr[mm].astype(F32)
        return carry

    lax.fori_loop(0, na - 1, gather_sum, 0)

    old = ua[m, pl.ds(q0, QR), :].astype(F32)
    ub[m, pl.ds(q0, QR), :] = (old - STEP_USER * (own_sum[...] + DECAY * old)).astype(BF16)

    def bz_copy(i):
        mm = peer(i)
        part = ub.at[m, pl.ds(q0, QR)]
        return rc(part, part, bz_s.at[mm], bz_r.at[m], zdev(mm))

    def send_new(i, carry):
        bz_copy(na - 2 - i).start()
        return carry

    lax.fori_loop(0, na - 1, send_new, 0)
    forward_y(ub, m, by_s, by_r)

    def expand(i, mm):
        users = ub[mm]
        for part in range(NO // NX):
            picks = [pick(mm, part * NX + q) for q in range(NX)]
            scores = nt(jnp.concatenate([t[2] for t in picks], axis=0), users)
            hs = []
            for q in range(NX):
                k = part * NX + q
                code, j, block, flat = picks[q]
                s = scores[q * BLK:(q + 1) * BLK]
                hit = (cr[mm, k:k + 1, :] & 255) - 1 == sub
                margin = jnp.maximum(1.0 + s * jnp.where(hit, -c, c), 0.0)
                hs.append((margin * jnp.where(hit, -invcol[k, j], flat)).astype(BF16))
            terms = nn(jnp.concatenate(hs, axis=0), users)
            for q in range(NX):
                k = part * NX + q
                slot[k, i + 1] = terms[q * BLK:(q + 1) * BLK] + slot[k, prv[k, i]]

    def second_pass(i, carry):
        @pl.when(jnp.logical_and(i > 0, i < na))
        def _():
            mm = source(na - 1 - i)
            arrive_z(ub, mm, bz_s, bz_r)
            forward_y(ub, mm, by_s, by_r)

        @pl.when(i >= LAG2)
        def _():
            mm = source(na - 1 - (i - LAG2))
            three(ub, mm, by_s, by_r).wait_recv()
            expand(i - LAG2, mm)

        return carry

    lax.fori_loop(0, na + LAG2, second_pass, 0)

    keep_u = pltpu.make_async_copy(ub.at[m], ou_ref.at[pl.ds(b0, BLK)], l_sem.at[0])
    keep_u.start()
    out_u = rc(ub.at[m], ou_ref.at[pl.ds(b0, BLK)], o_s.at[0], o_r.at[0], sib)
    out_u.start()

    def item_sum(k, b):
        return slot[k, lst[k, b]]

    def core_copy(k):
        return rc(cs.at[k], ccr.at[k], g_s.at[k], g_r.at[k], sib)

    def other_half(k):
        for b in range(HB):
            cs[k, b * BLK:(b + 1) * BLK, :] = item_sum(k, o0 + b).astype(BF16)
        core_copy(k).start()

    def both(k):
        core_copy(k).wait_recv()
        for b in range(HB):
            rows = slice(b * BLK, (b + 1) * BLK)
            xs[k, rows, :] = (item_sum(k, h0 + b) + ccr[k, rows, :].astype(F32)).astype(BF16)

    def w_copy(xx):
        return rc(xs.at[far + xx, pl.ds(0, ZROWS)], zrec.at[xx], w_s.at[xx], w_r.at[xx], mate)

    def w_in(xx):
        return rc(xs.at[own + xx, pl.ds(0, ZROWS)], zrec.at[xx], w_s.at[xx], w_r.at[xx], mate)

    def v_copy(xx):
        return rc(xs.at[far + xx, pl.ds(ZROWS, HALF - ZROWS)], xrec1.at[x], v_s.at[xx], v_r.at[x], xdev(xx))

    def xa_copy(xx):
        rows = pl.ds(ZROWS, HALF - ZROWS)
        return rc(xs.at[own + xx, rows], xrec.at[x, rows], x_s.at[xx], x_r.at[x], xdev(xx))

    def xb_copy(xx):
        rows = pl.ds(0, ZROWS)
        return rc(xs.at[own + xx, rows], xrec.at[x, rows], xb_s.at[xx], xb_r.at[x], xdev(xx))

    order = [off(x, d, NX) for d in (2, 1, 3, 0)]
    owners = [far + xx for xx in order] + [own + xx for xx in order]
    other_half(owners[0])
    other_half(owners[1])
    for n, k in enumerate(owners):
        if n + 2 < NO:
            other_half(owners[n + 2])
        both(k)
        xx = order[n % NX]
        if n < NX:
            w_copy(xx).start()
            if n < NX - 1:
                v_copy(xx).start()
        elif n < NO - 1:
            xa_copy(xx).start()

    for n, xx in enumerate(order):
        k = own + xx
        w_in(xx).wait_recv()
        rows = pl.ds(0, ZROWS)
        xs[k, rows, :] = (xs[k, rows, :].astype(F32) + zrec[xx].astype(F32)).astype(BF16)
        if n < NX - 1:
            xb_copy(xx).start()

    part = xs[far + x, pl.ds(ZROWS, HALF - ZROWS), :].astype(F32)
    for d in (1, 3, 2):
        xx = off(x, d, NX)
        rc(xrec1.at[xx], xrec1.at[xx], v_s.at[xx], v_r.at[xx], xdev(xx)).wait_recv()
        part = part + xrec1[xx].astype(F32)
    psum[...] = part.astype(BF16)
    to_mate = rc(psum, prec, t_s, t_r, mate)
    to_mate.start()

    for d in (1, 3, 2):
        xx = off(x, d, NX)
        lower, upper = xrec.at[xx, pl.ds(0, ZROWS)], xrec.at[xx, pl.ds(ZROWS, HALF - ZROWS)]
        rc(upper, upper, x_s.at[xx], x_r.at[xx], xdev(xx)).wait_recv()
        rc(lower, lower, xb_s.at[xx], xb_r.at[xx], xdev(xx)).wait_recv()
    to_mate.wait_recv()
    def out_item(b, start):
        return rc(fin.at[b], oi_ref.at[start + b], o_s.at[1 + b], o_r.at[1 + b], sib)

    def keep_item(b):
        return pltpu.make_async_copy(fin.at[b], oi_ref.at[h0 + b], l_sem.at[1 + b])

    for b in range(2 * HB):
        rows = pl.ds(b * CUT, CUT)
        total = xs[k0, rows, :].astype(F32)
        for d in range(1, NX):
            total = total + xrec[off(x, d, NX), rows, :].astype(F32)
        if b * CUT >= ZROWS:
            total = total + prec[pl.ds(b * CUT - ZROWS, CUT), :].astype(F32)
        piece = pl.ds(b % 2 * CUT, CUT)
        olds = items[k0, h0 + b // 2, piece, :].astype(F32)
        fin[b // 2, piece, :] = (olds - STEP_ITEM * (total + DECAY * olds)).astype(BF16)
        if b % 2:
            out_item(b // 2, h0).start()
            keep_item(b // 2).start()

    iz_copy(k0).wait_send()
    pz_copy(k0).wait_send()
    to_mate.wait_send()
    core_items(far + x, h0).wait_send()
    for d in range(NX):
        xx = off(x, d, NX)
        core_copy(own + xx).wait_send()
        core_copy(far + xx).wait_send()
        w_copy(xx).wait_send()
        if d:
            ix_copy(xx).wait_send()
            jx_copy(xx).wait_send()
            jz_copy(own + xx, xx).wait_send()
            core_items(own + xx, h0).wait_send()
            core_far(xx, h0, True).wait_send()
            core_far(xx, h0, False).wait_send()
            p_copy(k0, xx, p_s, p_r, x).wait_send()
            p_copy(far + x, xx, pf_s, pf_r, x).wait_send()
            v_copy(xx).wait_send()
            xa_copy(xx).wait_send()
            xb_copy(xx).wait_send()

    def sent(i, carry):
        code_copy(i).wait_send()
        az_copy(i).wait_send()
        bz_copy(i).wait_send()
        mm = peer(i)
        three(ua, mm, ay_s, ay_r).wait_send()
        rz_copy(mm).wait_send()
        return carry

    lax.fori_loop(0, na - 1, sent, 0)

    def sent_all(i, carry):
        three(ub, i, by_s, by_r).wait_send()
        three(gs, i, ry_s, ry_r).wait_send()
        return carry

    lax.fori_loop(0, na, sent_all, 0)
    out_u.wait_send()
    keep_u.wait()
    other_b = pl.multiple_of((1 - r) * BLK, BLK)
    rc(ub.at[m], ou_ref.at[pl.ds(other_b, BLK)], o_s.at[0], o_r.at[0], sib).wait_recv()
    for b in range(HB):
        keep_item(b).wait()
        out_item(b, h0).wait_send()
        out_item(b, o0).wait_recv()


def hand_over(u_ref, i_ref, ou_ref, oi_ref):
    ou_ref[...] = u_ref[...]
    oi_ref[...] = i_ref[...]


def body(na, user_factors, item_factors, item_bucket, propensity, tile_blocks, positives):
    dma = pltpu.SemaphoreType.DMA
    V = pltpu.VMEM
    scratch = [
        V((IBD, BLK), jnp.int32),
        pltpu.SMEM((1, propensity.shape[0]), F32),
        V(tile_blocks.shape, jnp.int32),
        V((positives.shape[1], positives.shape[0]), jnp.int32),
        V((na, NO, BLK), jnp.int32),
        V((na, NO, BLK), jnp.int32),
        V((na, BLK), jnp.int32),
        pltpu.SMEM((na, BLK), jnp.int32),
        V((NO, IBD, BLK, RANK), BF16),
        V((NO, 8, BLK), F32),
        V((NO, IBD, 8, BLK), F32),
        V((NO, IBD, BLK, BLK), F32),
        V((na, BLK, RANK), BF16),
        V((na, BLK, RANK), BF16),
        V((na, BLK, RANK), BF16),
        V((na, BLK, RANK), BF16),
        V((na, QR, RANK), BF16),
        V((na, QR, RANK), BF16),
        V((NO, na + 1, BLK, RANK), F32),
        pltpu.SMEM((NO, na), jnp.int32),
        pltpu.SMEM((NO, IBD), jnp.int32),
        V((NO, HALF, RANK), BF16),
        V((NO, HALF, RANK), BF16),
        V((NO, HALF, RANK), BF16),
        V((NX, ZROWS, RANK), BF16),
        V((NX, HALF, RANK), BF16),
        V((NX, HALF - ZROWS, RANK), BF16),
        V((HALF - ZROWS, RANK), BF16),
        V((HALF - ZROWS, RANK), BF16),
        V((QR, RANK), F32),
        V((HB, BLK, RANK), BF16),
        dma((na,)), dma((na,)), dma,
        dma((NX,)), dma((NX,)), dma, dma, dma((NX,)), dma((NX,)), dma((NX,)), dma((NX,)), dma((NO,)), dma((NO,)),
        dma((NX,)), dma((NX,)),
        dma((NX,)), dma((NX,)), dma, dma, dma((NX,)), dma((NX,)),
        dma((na,)), dma((na,)), dma((na,)), dma((na,)),
        dma((na,)), dma((na,)), dma((na,)), dma((na,)),
        dma((na,)), dma((na,)), dma((na,)), dma((na,)),
        dma((NO,)), dma((NO,)), dma((NX,)), dma((NX,)), dma((NX,)), dma((NX,)),
        dma((NX,)), dma((NX,)), dma((NX,)), dma((NX,)), dma, dma,
        dma((1 + HB,)), dma((1 + HB,)), dma((6,)),
    ]
    vmem = pl.BlockSpec(memory_space=pltpu.VMEM)
    anywhere = pl.BlockSpec(memory_space=pl.ANY)
    new_users, new_items = pl.pallas_call(
        functools.partial(kernel, na),
        out_shape=(
            jax.ShapeDtypeStruct(user_factors.shape, BF16),
            jax.ShapeDtypeStruct((IBD, BLK, RANK), BF16),
        ),
        in_specs=[anywhere] * 6,
        out_specs=(anywhere, anywhere),
        scratch_shapes=scratch,
        compiler_params=pltpu.CompilerParams(
            collective_id=0, has_side_effects=True, vmem_limit_bytes=56 << 20),
    )(
        user_factors,
        item_factors.reshape(IBD, BLK, RANK),
        item_bucket.reshape(IBD, BLK),
        propensity.reshape(1, -1),
        tile_blocks,
        positives.T,
    )
    new_users, new_items = pl.pallas_call(
        hand_over,
        out_shape=(
            jax.ShapeDtypeStruct(user_factors.shape, BF16),
            jax.ShapeDtypeStruct((IBD, BLK, RANK), BF16),
        ),
        in_specs=[vmem, vmem],
        out_specs=(vmem, vmem),
    )(new_users, new_items)
    return new_users, new_items.reshape(item_factors.shape)


def solution(mesh):
    na = mesh.shape["user"] // NX // 2
    return jax.shard_map(
        functools.partial(body, na),
        mesh=mesh,
        in_specs=(
            P("user", None),
            P(("user", "item"), None),
            P(("user", "item")),
            P(),
            P("user", "item"),
            P("user", "item"),
        ),
        out_specs=(P("user", None), P(("user", "item"), None)),
        check_vma=False,
    )
```
